256 devices in a mesh: seq: 64 (over y_hi, x, z), head: 4 (over y_lo, core).
Axes of the slice: x: 4, y: 4 (y_hi: 2, y_lo: 2; y = y_hi * 2 + y_lo), z: 8, core: 2. Of those that a mesh axis runs over, the one named last changes fastest.
Arguments:
- query_in: bfloat16 [8192, 1024], P('seq', 'head'), may hold values from -180 to 180
- key_in: bfloat16 [8192, 1024], P('seq', 'head'), may hold values from -4.6 to 4.6
- value_in: bfloat16 [8192, 1024], P('seq', 'head'), may hold values from -6 to 6
- grad_out: bfloat16 [8192, 1024], P('seq', 'head'), may hold values from -6 to 6
- embedding: bfloat16 [8192, 64], P('seq'), may hold values from -1.1953125 to 1.1953125
- bias_gain: float32 [16], P('head'), may hold values from 0.5 to 2
Outputs:
- grad_query: bfloat16 [8192, 1024], P('seq', 'head')
- grad_key: bfloat16 [8192, 1024], P('seq', 'head')
- grad_value: bfloat16 [8192, 1024], P('seq', 'head')
- grad_embedding: float32 [8192, 64], P('seq')
The draws below stay inside these ranges and needn't reach their ends.
All inputs are finite; a program needn't handle non-finite values.
Results may differ from the reference program's by a relative error of at most 0.013.
Values may be sent and summed in bfloat16 or wider, within the bound.
A program may use at most 64 MiB of HBM per device.

```python
import math
import jax
import jax.numpy as jnp
from jax import lax

HEADS = 16
HEAD_DIM = 64
EMB = 64
WIDTH = 1024
NODES = 8192


def base_keys(key):
    return jnp.clip(jax.random.normal(key, (NODES, WIDTH), jnp.float32), -4.5, 4.5)


def draw_key_in(key, part):
    base_rows = base_keys(key)
    return base_rows.astype(jnp.bfloat16)


def draw_query_in(key, part):
    key = jax.random.fold_in(key, 23)
    drawn = jnp.clip(jax.random.normal(key, (NODES, WIDTH), jnp.float32), -4.5, 4.5)
    return drawn.astype(jnp.bfloat16)


def steps_of(key, dims, shards, low, top_value):
    factor_of = 1.0
    for dim, shards_of in shards:
        draws = jax.random.uniform(jax.random.fold_in(jax.random.fold_in(key, 6), dim), (shards_of,), jnp.float32, low / len(shards), top_value / len(shards))
        factor_of = factor_of * jnp.repeat(jnp.exp(draws), dims[dim] // shards_of).reshape((-1,) + (1,) * (len(dims) - 1 - dim))
    return factor_of


def centred(stream_key, extent, width, reach, cuts=(), kind=jnp.bfloat16):
    array = jax.random.normal(stream_key, extent, jnp.float32) * width
    if len(cuts) > 0:
        array = steps_of(stream_key, extent, cuts, -0.22, 0.18) * array
    return jnp.clip(array, min=-reach, max=reach).astype(kind)


def setup_inputs(seed: int = 0) -> dict:
    seeds = jax.random.split(jax.random.key(seed), 7)
    query_in = draw_query_in(jax.random.fold_in(seeds[6], 71), 0)
    key_in = draw_key_in(jax.random.fold_in(seeds[6], 71), 0)
    value_in = centred(seeds[2], (NODES, WIDTH), 1.0, 6.0, ((0, 64), (1, 4)))
    grad_out = centred(seeds[3], (NODES, WIDTH), 1.0, 6.0, ((0, 64), (1, 4)))
    embedding = centred(seeds[4], (NODES, EMB), 0.2, 1.1953125, ((0, 64),))
    bias_gain = jnp.clip(jnp.exp(math.log(2.0) - 1.3862944 * jax.random.uniform(seeds[5], (HEADS,), jnp.float32) ** steps_of(seeds[5], (HEADS,), ((0, 4),), -0.2, 0.2)), 0.5, 2.0)
    return {"query_in": query_in, "key_in": key_in, "value_in": value_in, "grad_out": grad_out, "embedding": embedding, "bias_gain": bias_gain}


def distances(left, right):
    cross = jnp.dot(left, right.T, precision=lax.Precision.HIGHEST, preferred_element_type=jnp.float32)
    left_sq = jnp.sum(left * left, axis=1)
    right_sq = jnp.sum(right * right, axis=1)
    return left_sq[:, None] + right_sq[None, :] - 2.0 * cross


def reference(query_in, key_in, value_in, grad_out, embedding, bias_gain):
    scaling = HEAD_DIM ** -0.5
    emb_full = embedding.astype(jnp.float32)
    distance = distances(emb_full, emb_full)

    def one_head(grad_bias, head_num):
        first_col = (head_num * HEAD_DIM).astype(jnp.int32)
        query_h = lax.dynamic_slice_in_dim(query_in, first_col, HEAD_DIM, 1)
        key_h = lax.dynamic_slice_in_dim(key_in, first_col, HEAD_DIM, 1)
        value_h = lax.dynamic_slice_in_dim(value_in, first_col, HEAD_DIM, 1)
        grad_h = lax.dynamic_slice_in_dim(grad_out, first_col, HEAD_DIM, 1)
        gain = bias_gain[head_num]
        scores = jnp.dot(query_h, key_h.T, preferred_element_type=jnp.float32) * scaling - gain * distance
        row_max = jnp.max(scores, axis=1, keepdims=True)
        log_total = row_max + jnp.log(jnp.sum(jnp.exp(scores - row_max), axis=1, keepdims=True))
        weights = jnp.exp(scores - log_total)
        attended = jnp.dot(weights, value_h.astype(jnp.float32), precision=lax.Precision.HIGHEST)
        row_delta = jnp.sum(grad_h.astype(jnp.float32) * attended, axis=1, keepdims=True)
        grad_prob = jnp.dot(grad_h, value_h.T, preferred_element_type=jnp.float32)
        grad_score = weights * (grad_prob - row_delta)
        score_half = grad_score.astype(jnp.bfloat16)
        weight_half = weights.astype(jnp.bfloat16)
        grad_q = (jnp.dot(score_half, key_h, preferred_element_type=jnp.float32) * scaling).astype(jnp.bfloat16)
        grad_k = (jnp.dot(score_half.T, query_h, preferred_element_type=jnp.float32) * scaling).astype(jnp.bfloat16)
        grad_v = jnp.dot(weight_half.T, grad_h, preferred_element_type=jnp.float32).astype(jnp.bfloat16)
        return grad_bias - gain * grad_score, (grad_q, grad_k, grad_v)

    start_bias = jnp.zeros((NODES, NODES), jnp.float32)
    grad_bias, stacked = lax.scan(one_head, start_bias, jnp.arange(HEADS, dtype=jnp.int32))
    stack_q, stack_k, stack_v = stacked
    grad_query = jnp.transpose(stack_q, (1, 0, 2)).reshape(NODES, WIDTH)
    grad_key = jnp.transpose(stack_k, (1, 0, 2)).reshape(NODES, WIDTH)
    grad_value = jnp.transpose(stack_v, (1, 0, 2)).reshape(NODES, WIDTH)
    paired = grad_bias + grad_bias.T
    pulled = jnp.dot(paired, emb_full, precision=lax.Precision.HIGHEST)
    grad_embedding = 2.0 * (jnp.sum(paired, axis=1)[:, None] * emb_full - pulled)
    return grad_query, grad_key, grad_value, grad_embedding
```

```python
import functools

import jax
import jax.numpy as jnp
from jax import lax
from jax.experimental import pallas as pl
from jax.experimental.pallas import tpu as pltpu
from jax.sharding import PartitionSpec as P

MESH = pl.DeviceIdType.MESH
F32 = jnp.float32
BF16 = jnp.bfloat16
LANES = 128
TILE = 256
ONE_LANE = 76
EMB_ROWS = 80


def nt_dot(left, right):
    return lax.dot_general(left, right, (((1,), (1,)), ((), ())), preferred_element_type=F32)


def nn_dot(left, right):
    return jnp.dot(left, right, preferred_element_type=F32)


def rounded(x):
    return x.astype(BF16).astype(F32)


def three_parts(x):
    first = rounded(x)
    second = rounded(x - first)
    return first, second, rounded(x - first - second)


def gain_pattern(base, gain):
    lane = lax.broadcasted_iota(jnp.int32, (1, LANES), 1) - base
    one, two, three = three_parts(jnp.full((1, LANES), gain, F32))
    out = jnp.where((lane == 0) | (lane == 3) | (lane == 5), -one, 0.0)
    out = jnp.where((lane == 1) | (lane == 4), -two, out)
    return jnp.where(lane == 2, -three, out)


Z_FIRST = ((0, 2, 2, 0), (0, -2, 6, 0), (0, 1, 1, 0), (0, -1, 7, 0))
Z_AHEAD = ((-2, 2, 4, 1), (-2, 1, 3, 0))
Z_BACK = ((2, -2, 0, 2), (2, -1, 5, 0))
FAR_FIRST = (4, 3, 5, 2, 6, 1, 7)


def kernel(
    na, nz, nh,
    gain_ref, q_ref, k_ref, v_ref, g_ref, emb_ref,
    dq_ref, dk_ref, dv_ref, de_ref,
    qd, kv, eq, ek, ka, qa, qx, ket, eqt, emb_q, emb_k, erq, erk,
    scores, probs, w16, d16, own_max, stats, combined,
    dqt, row_emb, col_emb, dq_out, dkv_out, dq_in, dkv_in,
    emb_out, emb_in, head_out, head_in,
    gz_send, gz_recv, ga_send, ga_recv, st_send, st_recv,
    dq_send, dq_recv, dkv_send, dkv_recv, em_send, em_recv, hd_send, hd_recv,
):
    rows = q_ref.shape[0]
    heads = q_ref.shape[1] // 64
    nq, nk = nz * rows, na * rows
    nx = na // 2
    last = heads - 1
    seq, head = lax.axis_index("seq"), lax.axis_index("head")
    a, z = seq // nz, seq % nz
    y, x = a // nx, a % nx
    own_q = pl.multiple_of(z * rows, rows)
    own_k = pl.multiple_of(a * rows, rows)

    def z_at(step):
        return (z + step + nz) % nz

    def z_device(place):
        return (a * nz + place, head)

    def a_device(place):
        return (place * nz + z, head)

    barrier = pltpu.get_barrier_semaphore()

    def greet(target):
        pl.semaphore_signal(barrier, inc=1, device_id=target, device_id_type=MESH)

    for step in range(1, nz):
        greet(z_device(z_at(step)))
    for step in range(1, na):
        greet(a_device((a + step) % na))
    for step in range(1, nh):
        greet((seq, (head + step) % nh))

    eq[:, pl.ds(own_q, rows)] = emb_ref[...]
    ek[:, pl.ds(own_k, rows)] = emb_ref[...]
    for h in range(heads):
        cols = slice(h * 64, (h + 1) * 64)
        qd[h, pl.ds(own_q, rows), :] = jnp.concatenate(
            [q_ref[:, cols].astype(F32) * 0.125, g_ref[:, cols].astype(F32)], axis=1
        ).astype(BF16)
        kv[h, pl.ds(own_k, rows), :] = jnp.concatenate(
            [k_ref[:, cols].astype(F32), v_ref[:, cols].astype(F32)], axis=1
        ).astype(BF16)

    pl.semaphore_wait(barrier, (nz - 1) + (na - 1) + (nh - 1))

    def piece(msg, buffer, emb_buffer, place, part):
        at = pl.multiple_of(place * rows, rows)
        if msg is None:
            size = 64 if part == 0 else 32
            return emb_buffer.at[pl.ds(32 if part == 2 else 0, size), pl.ds(at, rows)]
        size = rows if part == 0 else rows // 2
        return buffer.at[msg, pl.ds(at + (rows // 2 if part == 2 else 0), size), :]

    def number(msg):
        return heads if msg is None else msg

    def z_send(msg, plan):
        for held, to, slot, part in plan:
            block = piece(msg, qd, eq, z_at(held), part)
            pltpu.make_async_remote_copy(
                src_ref=block, dst_ref=block,
                send_sem=gz_send.at[number(msg)], recv_sem=gz_recv.at[number(msg), slot],
                device_id=z_device(z_at(to)), device_id_type=MESH).start()

    def z_wait(msg, slot):
        block = piece(msg, qd, eq, z_at(-4 if slot == 0 else -slot), {0: 2, 4: 1}.get(slot, 0))
        pltpu.make_async_copy(block, block, gz_recv.at[number(msg), slot]).wait()

    def a_send(msg, partner):
        held = ((y + partner) % 2) * nx + x
        block = piece(msg, kv, ek, held, 0)
        targets = [] if partner else [(4, ((y + 1) % 2) * nx + x)]
        targets += [(4 * partner + step, y * nx + (x + step) % nx) for step in (2, 1, 3)]
        for slot, place in targets:
            pltpu.make_async_remote_copy(
                src_ref=block, dst_ref=block,
                send_sem=ga_send.at[number(msg)], recv_sem=ga_recv.at[number(msg), slot],
                device_id=a_device(place), device_id_type=MESH).start()

    def a_wait(msg, slot):
        held = ((y + slot // 4) % 2) * nx + (x - slot % 4 + nx) % nx
        block = piece(msg, kv, ek, held, 0)
        pltpu.make_async_copy(block, block, ga_recv.at[number(msg), slot]).wait()

    def gather_start(msg):
        a_send(msg, 0)
        z_send(msg, Z_FIRST)

    def gather_forward(msg):
        a_wait(msg, 4)
        a_send(msg, 1)
        z_wait(msg, 2)
        z_send(msg, Z_AHEAD)
        z_wait(msg, 6)
        z_send(msg, Z_BACK)

    def gather_end(msg):
        for slot in (1, 7, 3, 5, 4, 0):
            z_wait(msg, slot)
        for slot in (1, 3, 2, 5, 7, 6):
            a_wait(msg, slot)

    def spread_z(source, dest, send_sem, recv_sem):
        for step in FAR_FIRST:
            other = z_at(step)
            pltpu.make_async_remote_copy(
                src_ref=source(other), dst_ref=dest, send_sem=send_sem, recv_sem=recv_sem,
                device_id=z_device(other), device_id_type=MESH).start()

    def send_a(other, source, dest, send_sem, recv_sem):
        @pl.when(other != a)
        def _():
            pltpu.make_async_remote_copy(
                src_ref=source, dst_ref=dest, send_sem=send_sem, recv_sem=recv_sem,
                device_id=a_device(other), device_id_type=MESH).start()

    def bytes_of(block, sem):
        pltpu.make_async_copy(block, block, sem).wait()

    gather_start(None)
    gather_start(0)
    row_emb[...] = jnp.zeros_like(row_emb)
    col_emb[...] = jnp.zeros_like(col_emb)
    gather_forward(None)
    gather_forward(0)
    gather_start(1)
    gather_end(None)

    def widened(emb_t, base):
        e = emb_t.astype(F32)
        one, two, three = three_parts(jnp.sum(e * e, axis=0, keepdims=True))
        row = lax.broadcasted_iota(jnp.int32, (16, e.shape[1]), 0) + (64 - base)
        extra = jnp.where((row >= 0) & (row < 3), one, 0.0)
        extra = jnp.where((row >= 3) & (row < 5), two, extra)
        extra = jnp.where(row == 5, three, extra)
        extra = jnp.where(row == ONE_LANE - base, 1.0, extra)
        return jnp.concatenate([e, extra, jnp.zeros((48, e.shape[1]), F32)], axis=0)

    eqt[...] = widened(eq[...], 64)
    emb_q[...] = jnp.transpose(eqt[...])
    wide_k = widened(ek[...], 70)
    ket[64:, :] = wide_k[:EMB_ROWS].astype(BF16)
    emb_k[...] = jnp.transpose(wide_k)
    qx[:, LANES:] = emb_q[...].astype(BF16)
    erq[...] = pltpu.roll(emb_q[...], 64, 1)
    erk[...] = pltpu.roll(emb_k[...], 64, 1).astype(BF16)

    low_lane = lax.broadcasted_iota(jnp.int32, (1, LANES), 1) < 64
    low_f32 = jnp.where(low_lane, 1.0, 0.0)
    high_f32 = 1.0 - low_f32

    def first_pass(h):
        slot = h % 2
        gather_end(h)
        gain = gain_ref[h]
        ka[:, :LANES] = (kv[h].astype(F32) * low_f32 + erk[...].astype(F32) * high_f32).astype(BF16)
        less = jnp.where(lax.broadcasted_iota(jnp.int32, (1, LANES), 1) == ONE_LANE, -1.0, 0.0)
        ka[:, LANES:] = (emb_k[...] + (gain_pattern(64, gain) + less)).astype(BF16)
        shifted = erq[...] * (2.0 * gain)
        scaled = emb_q[...] * (2.0 * gain)
        qa[:, :LANES] = (qd[h].astype(F32) * low_f32 + rounded(shifted) * high_f32).astype(BF16)
        low_part = scaled - rounded(scaled)
        qa[:, LANES:] = (
            low_part * low_f32 + (emb_q[...] + gain_pattern(70, gain)) * high_f32
        ).astype(BF16)

        def block(qb, _):
            at = pl.multiple_of(qb * TILE, TILE)
            q_tile = qa[pl.ds(at, TILE), :]
            top = jnp.full((8, TILE), -jnp.inf, F32)
            for kb in range(nk // TILE):
                s = nt_dot(ka[kb * TILE:(kb + 1) * TILE, :], q_tile)
                scores[slot, kb * TILE:(kb + 1) * TILE, pl.ds(at, TILE)] = s
                top = jnp.maximum(top, jnp.max(s.reshape(TILE // 8, 8, TILE), axis=0))
            top = jnp.max(top, axis=0, keepdims=True)
            g_tile = (qd[h, pl.ds(at, TILE), :].astype(F32) * high_f32).astype(BF16)
            total = jnp.zeros((8, TILE), F32)
            moment = jnp.zeros((8, TILE), F32)
            for kb in range(nk // TILE):
                keys = slice(kb * TILE, (kb + 1) * TILE)
                e = jnp.exp(scores[slot, keys, pl.ds(at, TILE)] - top)
                p = nt_dot(kv[h, keys, :], g_tile)
                scores[slot, keys, pl.ds(at, TILE)] = e
                probs[slot, keys, pl.ds(at, TILE)] = p
                total = total + jnp.sum(e.reshape(TILE // 8, 8, TILE), axis=0)
                moment = moment + jnp.sum((e * p).reshape(TILE // 8, 8, TILE), axis=0)
            total = jnp.sum(total, axis=0, keepdims=True)
            moment = jnp.sum(moment, axis=0, keepdims=True) / total
            log_sum = top + jnp.log(total)
            for part in range(TILE // LANES):
                cols = slice(part * LANES, (part + 1) * LANES)
                row = qb * (TILE // LANES) + part
                own_max[slot, pl.ds(row, 1), :] = top[:, cols]
                stats[h, z, pl.ds(row, 1), :] = log_sum[:, cols]
                stats[h, z, pl.ds(row + 8, 1), :] = moment[:, cols]

            @pl.when((qb == 2) & (h < last))
            def _():
                gather_forward(h + 1)

            @pl.when((qb == 3) & (h < last - 1))
            def _():
                gather_start(h + 2)
            return 0

        lax.fori_loop(0, nq // TILE, block, 0)
        own = stats.at[h, z]
        spread_z(lambda other: own, own, st_send.at[h], st_recv.at[h])

    def second_pass(h):
        slot = h % 2
        gain = gain_ref[h]
        qx[:, :LANES] = qd[h]
        ket[:64, :] = jnp.transpose(kv[h].astype(F32))[:64].astype(BF16)
        dqt[...] = jnp.zeros_like(dqt)
        bytes_of(stats.at[h, pl.ds(0, nz - 1)], st_recv.at[h])
        top = stats[h, 0, 0:8, :]
        for other in range(1, nz):
            top = jnp.maximum(top, stats[h, other, 0:8, :])
        total = jnp.zeros((8, LANES), F32)
        moment = jnp.zeros((8, LANES), F32)
        for other in range(nz):
            share = jnp.exp(stats[h, other, 0:8, :] - top)
            total = total + share
            moment = moment + stats[h, other, 8:16, :] * share
        combined[0:8, :] = jnp.exp(own_max[slot] - top) / total
        combined[8:16, :] = moment / total

        def block(kb, _):
            at = pl.multiple_of(kb * TILE, TILE)
            for part in range(nq // LANES):
                cols = slice(part * LANES, (part + 1) * LANES)
                w = scores[slot, pl.ds(at, TILE), cols] * combined[part:part + 1, :]
                d = w * (probs[slot, pl.ds(at, TILE), cols] - combined[8 + part:9 + part, :])
                w16[:, cols] = w.astype(BF16)
                d16[:, cols] = d.astype(BF16)
            grad_v = nn_dot(w16[...], qx[:, :LANES])
            grad_k = nn_dot(d16[...], qx[...])
            dkv_out[h, pl.ds(at, TILE), :] = (
                grad_k[:, :LANES] * low_f32 + grad_v * high_f32
            ).astype(BF16)
            col_emb[pl.ds(at, TILE), :] += gain * grad_k[:, LANES:]
            for part in range(TILE // rows):
                other = kb * (TILE // rows) + part
                send_a(other, dkv_out.at[h, pl.ds(at + part * rows, rows), :], dkv_in.at[h, a],
                       dkv_send.at[h], dkv_recv.at[h])

            @pl.when(h == last)
            def _():
                col_t = jnp.transpose(col_emb[pl.ds(at, TILE), :])
                emb_out[1, :, pl.ds(at, TILE)] = (-2.0 * (
                    col_t[ONE_LANE:ONE_LANE + 1, :] * ek[:, pl.ds(at, TILE)].astype(F32)
                    - col_t[:64, :])).astype(BF16)
                for part in range(TILE // rows):
                    other = kb * (TILE // rows) + part
                    send_a(other, emb_out.at[1, :, pl.ds(at + part * rows, rows)],
                           emb_in.at[1, a], em_send.at[1], em_recv.at[1])
            dqt[...] += nn_dot(ket[:, pl.ds(at, TILE)], d16[...])
            return 0

        lax.fori_loop(0, nk // TILE, block, 0)
        row_emb[...] += gain * dqt[64:, :]

        @pl.when(h == last)
        def _():
            emb_out[0] = (-2.0 * (
                row_emb[ONE_LANE:ONE_LANE + 1, :] * eqt[:64, :] - row_emb[:64, :])).astype(BF16)
            spread_z(
                lambda other: emb_out.at[0, :, pl.ds(pl.multiple_of(other * rows, rows), rows)],
                emb_in.at[0, z], em_send.at[0], em_recv.at[0])

        dq_out[h] = (dqt[:64, :] * 0.125).astype(BF16)
        spread_z(
            lambda other: dq_out.at[h, :, pl.ds(pl.multiple_of(other * rows, rows), rows)],
            dq_in.at[h, z], dq_send.at[h], dq_recv.at[h])
        dq_in[h, z] = dq_out[h, :, pl.ds(own_q, rows)]
        dkv_in[h, a] = dkv_out[h, pl.ds(own_k, rows), :]

    def step(t, _):
        @pl.when(t < heads)
        def _():
            first_pass(t)

        @pl.when(t > 0)
        def _():
            second_pass(t - 1)
        return 0

    lax.fori_loop(0, heads + 1, step, 0)
    emb_in[0, z] = emb_out[0, :, pl.ds(own_q, rows)]
    emb_in[1, a] = emb_out[1, :, pl.ds(own_k, rows)]

    def reduce_pair(pair):
        halves = []
        for h in (2 * pair, 2 * pair + 1):
            bytes_of(dq_in.at[h, pl.ds(0, nz - 1)], dq_recv.at[h])
            bytes_of(dkv_in.at[h, pl.ds(0, na - 1)], dkv_recv.at[h])
            halves.append((
                jnp.sum(dq_in[h].astype(F32), axis=0), jnp.sum(dkv_in[h].astype(F32), axis=0)))
        cols = slice(pair * LANES, (pair + 1) * LANES)
        (q0, kv0), (q1, kv1) = halves
        dq_ref[:, cols] = jnp.transpose(jnp.concatenate([q0, q1], axis=0)).astype(BF16)
        dk_ref[:, cols] = jnp.concatenate([kv0[:, :64], kv1[:, :64]], axis=1).astype(BF16)
        dv_ref[:, cols] = jnp.concatenate([kv0[:, 64:], kv1[:, 64:]], axis=1).astype(BF16)

    def gather_sent(msg):
        whole_q, whole_k = (eq, ek) if msg is None else (qd.at[msg], kv.at[msg])
        if msg is None:
            whole_q, whole_k = eq.at[:, pl.ds(0, nq - rows)], ek.at[:, pl.ds(0, nk - rows)]
        else:
            whole_q = qd.at[msg, pl.ds(0, nq - rows), :]
            whole_k = kv.at[msg, pl.ds(0, nk - rows), :]
        bytes_of(whole_q, gz_send.at[number(msg)])
        bytes_of(whole_k, ga_send.at[number(msg)])

    for pair in range(heads // 2 - 1):
        reduce_pair(pair)
    gather_sent(None)
    for h in range(heads):
        gather_sent(h)
        bytes_of(stats.at[h, pl.ds(0, nz - 1)], st_send.at[h])
    bytes_of(emb_in.at[1, pl.ds(0, na - 1)], em_recv.at[1])
    bytes_of(emb_in.at[0, pl.ds(0, nz - 1)], em_recv.at[0])
    mine = jnp.sum(emb_in[0].astype(F32), axis=0) + jnp.sum(emb_in[1].astype(F32), axis=0)
    head_out[...] = mine
    for step in range(1, nh):
        pltpu.make_async_remote_copy(
            src_ref=head_out, dst_ref=head_in.at[head], send_sem=hd_send, recv_sem=hd_recv,
            device_id=(seq, (head + step) % nh), device_id_type=MESH).start()
    head_in[head] = mine
    reduce_pair(heads // 2 - 1)
    for h in range(heads):
        bytes_of(dq_in.at[h, pl.ds(0, nz - 1)], dq_send.at[h])
        bytes_of(dkv_in.at[h, pl.ds(0, na - 1)], dkv_send.at[h])
    bytes_of(emb_in.at[0, pl.ds(0, nz - 1)], em_send.at[0])
    bytes_of(emb_in.at[1, pl.ds(0, na - 1)], em_send.at[1])
    bytes_of(head_in.at[pl.ds(0, nh - 1)], hd_send)
    bytes_of(head_in.at[pl.ds(0, nh - 1)], hd_recv)
    de_ref[...] = jnp.sum(head_in[...], axis=0)


def on_device(na, nz, nh, query_in, key_in, value_in, grad_out, embedding, bias_gain):
    rows, width = query_in.shape
    heads = width // 64
    nq, nk = nz * rows, na * rows
    vmem = pl.BlockSpec(memory_space=pltpu.VMEM)
    dma = pltpu.SemaphoreType.DMA
    grad_q, grad_k, grad_v, grad_e = pl.pallas_call(
        functools.partial(kernel, na, nz, nh),
        out_shape=(
            jax.ShapeDtypeStruct((rows, width), BF16),
            jax.ShapeDtypeStruct((rows, width), BF16),
            jax.ShapeDtypeStruct((rows, width), BF16),
            jax.ShapeDtypeStruct((64, rows), F32),
        ),
        in_specs=[pl.BlockSpec(memory_space=pltpu.SMEM)] + [vmem] * 5,
        out_specs=(vmem,) * 4,
        scratch_shapes=[
            pltpu.VMEM((heads, nq, LANES), BF16),
            pltpu.VMEM((heads, nk, LANES), BF16),
            pltpu.VMEM((64, nq), BF16),
            pltpu.VMEM((64, nk), BF16),
            pltpu.VMEM((nk, 2 * LANES), BF16),
            pltpu.VMEM((nq, 2 * LANES), BF16),
            pltpu.VMEM((nq, 2 * LANES), BF16),
            pltpu.VMEM((64 + EMB_ROWS, nk), BF16),
            pltpu.VMEM((LANES, nq), F32),
            pltpu.VMEM((nq, LANES), F32),
            pltpu.VMEM((nk, LANES), F32),
            pltpu.VMEM((nq, LANES), F32),
            pltpu.VMEM((nk, LANES), BF16),
            pltpu.VMEM((2, nk, nq), F32),
            pltpu.VMEM((2, nk, nq), F32),
            pltpu.VMEM((TILE, nq), BF16),
            pltpu.VMEM((TILE, nq), BF16),
            pltpu.VMEM((2, 8, LANES), F32),
            pltpu.VMEM((heads, nz, 16, LANES), F32),
            pltpu.VMEM((16, LANES), F32),
            pltpu.VMEM((64 + EMB_ROWS, nq), F32),
            pltpu.VMEM((EMB_ROWS, nq), F32),
            pltpu.VMEM((nk, LANES), F32),
            pltpu.VMEM((heads, 64, nq), BF16),
            pltpu.VMEM((heads, nk, LANES), BF16),
            pltpu.VMEM((heads, nz, 64, rows), BF16),
            pltpu.VMEM((heads, na, rows, LANES), BF16),
            pltpu.VMEM((2, 64, max(nq, nk)), BF16),
            pltpu.VMEM((2, max(na, nz), 64, rows), BF16),
            pltpu.VMEM((64, rows), F32),
            pltpu.VMEM((nh, 64, rows), F32),
            dma((heads + 1,)), dma((heads + 1, nz)),
            dma((heads + 1,)), dma((heads + 1, na)),
            dma((heads,)), dma((heads,)),
            dma((heads,)), dma((heads,)),
            dma((heads,)), dma((heads,)),
            dma((2,)), dma((2,)),
            dma, dma,
        ],
        compiler_params=pltpu.CompilerParams(
            collective_id=0, has_side_effects=True, vmem_limit_bytes=56 * 1024 * 1024
        ),
    )(bias_gain, query_in, key_in, value_in, grad_out, embedding.T)
    return grad_q, grad_k, grad_v, grad_e.T


def solution(mesh):
    seq, nh = mesh.shape["seq"], mesh.shape["head"]
    nz = 1
    while nz * nz < seq:
        nz *= 2
    na = seq // nz
    placed = (
        P("seq", "head"),
        P("seq", "head"),
        P("seq", "head"),
        P("seq", "head"),
        P("seq", None),
        P("head"),
    )
    return jax.shard_map(
        functools.partial(on_device, na, nz, nh),
        mesh=mesh,
        in_specs=placed,
        out_specs=(P("seq", "head"), P("seq", "head"), P("seq", "head"), P("seq", None)),
        check_vma=False,
    )
```

```python
import functools

import jax
import jax.numpy as jnp
from jax import lax
from jax.experimental import pallas as pl
from jax.experimental.pallas import tpu as pltpu
from jax.sharding import PartitionSpec as P

MESH = pl.DeviceIdType.MESH
F32 = jnp.float32
BF16 = jnp.bfloat16
LANES = 128
TILE = 256
ONE_LANE = 76
SLOTS = 3
EMB_ROWS = 80


def nt_dot(left, right):
    return lax.dot_general(left, right, (((1,), (1,)), ((), ())), preferred_element_type=F32)


def nn_dot(left, right):
    return jnp.dot(left, right, preferred_element_type=F32)


def rounded(x):
    return x.astype(BF16).astype(F32)


def three_parts(x):
    first = rounded(x)
    second = rounded(x - first)
    return first, second, rounded(x - first - second)


def gain_pattern(base, gain):
    lane = lax.broadcasted_iota(jnp.int32, (1, LANES), 1) - base
    one, two, three = three_parts(jnp.full((1, LANES), gain, F32))
    out = jnp.where((lane == 0) | (lane == 3) | (lane == 5), -one, 0.0)
    out = jnp.where((lane == 1) | (lane == 4), -two, out)
    return jnp.where(lane == 2, -three, out)


Z_FIRST = ((0, 2, 2, 0), (0, -2, 6, 0), (0, 1, 1, 0), (0, -1, 7, 0))
Z_AHEAD = ((-2, 2, 4, 1), (-2, 1, 3, 0))
Z_BACK = ((2, -2, 0, 2), (2, -1, 5, 0))
FAR_FIRST = (4, 3, 5, 2, 6, 1, 7)


def kernel(
    na, nz, nh,
    gain_ref, q_ref, k_ref, v_ref, g_ref, emb_ref,
    dq_ref, dk_ref, dv_ref, de_ref,
    q_in, k_in, v_in, g_in, emb_in_place, in_sem,
    qd, kv, eq, ek, ka, qa, gq, qx, ket, eqt, twice_q, tail_q, tail_k,
    scores, probs, wd16, block_max, totals, moments, shares, stats, combined,
    row_emb, col_emb, dq_out, dkv_out, dq_in, dkv_in,
    emb_out, emb_in, head_out, head_in,
    gz_send, gz_recv, ga_send, ga_recv, st_send, st_recv,
    dq_send, dq_recv, dkv_send, dkv_recv, em_send, em_recv, hd_send, hd_recv,
):
    rows = q_ref.shape[0]
    heads = q_ref.shape[1] // 64
    nq, nk = nz * rows, na * rows
    nx = na // 2
    last = heads - 1
    seq, head = lax.axis_index("seq"), lax.axis_index("head")
    a, z = seq // nz, seq % nz
    y, x = a // nx, a % nx
    own_q = pl.multiple_of(z * rows, rows)
    own_k = pl.multiple_of(a * rows, rows)

    def z_at(step):
        return (z + step + nz) % nz

    def z_device(place):
        return (a * nz + place, head)

    def a_device(place):
        return (place * nz + z, head)

    barrier = pltpu.get_barrier_semaphore()

    def greet(target):
        pl.semaphore_signal(barrier, inc=1, device_id=target, device_id_type=MESH)

    for step in range(1, nz):
        greet(z_device(z_at(step)))
    for step in range(1, na):
        greet(a_device((a + step) % na))
    for step in range(1, nh):
        greet((seq, (head + step) % nh))

    loads = [
        pltpu.make_async_copy(source, dest, in_sem.at[i])
        for i, (source, dest) in enumerate((
            (emb_ref, emb_in_place), (q_ref, q_in), (g_ref, g_in), (k_ref, k_in), (v_ref, v_in)))
    ]
    for load in loads:
        load.start()
    for load in loads:
        load.wait()

    eq[:, pl.ds(own_q, rows)] = emb_in_place[...]
    ek[:, pl.ds(own_k, rows)] = emb_in_place[...]
    for h in range(heads):
        cols = slice(h * 64, (h + 1) * 64)
        qd[h, pl.ds(own_q, rows), :] = jnp.concatenate(
            [q_in[:, cols].astype(F32) * 0.125, g_in[:, cols].astype(F32)], axis=1
        ).astype(BF16)
        kv[h, pl.ds(own_k, rows), :] = jnp.concatenate(
            [k_in[:, cols].astype(F32), v_in[:, cols].astype(F32)], axis=1
        ).astype(BF16)

    pl.semaphore_wait(barrier, (nz - 1) + (na - 1) + (nh - 1))

    def piece(msg, buffer, emb_buffer, place, part):
        at = pl.multiple_of(place * rows, rows)
        if msg is None:
            size = 64 if part == 0 else 32
            return emb_buffer.at[pl.ds(32 if part == 2 else 0, size), pl.ds(at, rows)]
        size = rows if part == 0 else rows // 2
        return buffer.at[msg, pl.ds(at + (rows // 2 if part == 2 else 0), size), :]

    def number(msg):
        return heads if msg is None else msg

    def z_send(msg, plan):
        for held, to, slot, part in plan:
            block = piece(msg, qd, eq, z_at(held), part)
            pltpu.make_async_remote_copy(
                src_ref=block, dst_ref=block,
                send_sem=gz_send.at[number(msg)], recv_sem=gz_recv.at[number(msg), slot],
                device_id=z_device(z_at(to)), device_id_type=MESH).start()

    def z_wait(msg, slot):
        block = piece(msg, qd, eq, z_at(-4 if slot == 0 else -slot), {0: 2, 4: 1}.get(slot, 0))
        pltpu.make_async_copy(block, block, gz_recv.at[number(msg), slot]).wait()

    def a_send(msg, partner):
        held = ((y + partner) % 2) * nx + x
        block = piece(msg, kv, ek, held, 0)
        targets = [] if partner else [(4, ((y + 1) % 2) * nx + x)]
        targets += [(4 * partner + step, y * nx + (x + step) % nx) for step in (2, 1, 3)]
        for slot, place in targets:
            pltpu.make_async_remote_copy(
                src_ref=block, dst_ref=block,
                send_sem=ga_send.at[number(msg)], recv_sem=ga_recv.at[number(msg), slot],
                device_id=a_device(place), device_id_type=MESH).start()

    def a_wait(msg, slot):
        held = ((y + slot // 4) % 2) * nx + (x - slot % 4 + nx) % nx
        block = piece(msg, kv, ek, held, 0)
        pltpu.make_async_copy(block, block, ga_recv.at[number(msg), slot]).wait()

    def gather_start(msg):
        a_send(msg, 0)
        z_send(msg, Z_FIRST)

    def gather_forward(msg):
        a_wait(msg, 4)
        a_send(msg, 1)
        z_wait(msg, 2)
        z_send(msg, Z_AHEAD)
        z_wait(msg, 6)
        z_send(msg, Z_BACK)

    def gather_end(msg):
        for slot in (1, 7, 3, 5, 4, 0):
            z_wait(msg, slot)
        for slot in (1, 3, 2, 5, 7, 6):
            a_wait(msg, slot)

    def spread_z(source, dest, send_sem, recv_sem):
        for step in FAR_FIRST:
            other = z_at(step)
            pltpu.make_async_remote_copy(
                src_ref=source(other), dst_ref=dest, send_sem=send_sem, recv_sem=recv_sem,
                device_id=z_device(other), device_id_type=MESH).start()

    def send_a(other, source, dest, send_sem, recv_sem):
        @pl.when(other != a)
        def _():
            pltpu.make_async_remote_copy(
                src_ref=source, dst_ref=dest, send_sem=send_sem, recv_sem=recv_sem,
                device_id=a_device(other), device_id_type=MESH).start()

    def bytes_of(block, sem):
        pltpu.make_async_copy(block, block, sem).wait()

    gather_start(None)
    gather_start(0)
    row_emb[...] = jnp.zeros_like(row_emb)
    col_emb[...] = jnp.zeros_like(col_emb)
    gather_forward(None)
    gather_forward(0)
    gather_start(1)
    gather_start(2)
    gather_end(None)

    def widened(emb_t, base):
        e = emb_t.astype(F32)
        one, two, three = three_parts(jnp.sum(e * e, axis=0, keepdims=True))
        row = lax.broadcasted_iota(jnp.int32, (16, e.shape[1]), 0) + (64 - base)
        extra = jnp.where((row >= 0) & (row < 3), one, 0.0)
        extra = jnp.where((row >= 3) & (row < 5), two, extra)
        extra = jnp.where(row == 5, three, extra)
        extra = jnp.where(row == ONE_LANE - base, 1.0, extra)
        return jnp.concatenate([e, extra, jnp.zeros((48, e.shape[1]), F32)], axis=0)

    low_lane = lax.broadcasted_iota(jnp.int32, (1, LANES), 1) < 64
    low_f32 = jnp.where(low_lane, 1.0, 0.0)
    high_f32 = 1.0 - low_f32
    low_16, high_16 = low_f32.astype(BF16), high_f32.astype(BF16)
    one_lane = jnp.where(lax.broadcasted_iota(jnp.int32, (1, LANES), 1) == ONE_LANE, 1.0, 0.0)

    eqt[...] = widened(eq[...], 64)
    wide_k = widened(ek[...], 70)
    ket[64:, :] = wide_k[:EMB_ROWS].astype(BF16)
    wide_q = jnp.transpose(eqt[...])
    wide_k = jnp.transpose(wide_k)
    qx[:, LANES:] = wide_q.astype(BF16)
    tail_q[...] = (wide_q * high_f32).astype(BF16)
    tail_k[...] = ((wide_k - one_lane) * high_f32).astype(BF16)
    wide_q, wide_k = wide_q * low_f32, wide_k * low_f32
    twice_q[...] = wide_q + pltpu.roll(wide_q, 64, 1)
    ka[:, LANES:] = (wide_k + pltpu.roll(wide_k, 64, 1)).astype(BF16)

    def first_pass(h):
        slot = h % SLOTS
        @pl.when(h > 0)
        def _():
            gather_end(h)

        gain = gain_ref[h]
        ka[:, :LANES] = kv[h] * low_16 + (tail_k[...] + gain_pattern(64, gain).astype(BF16))
        qa[:, :LANES] = qd[h] * low_16 + (tail_q[...] + gain_pattern(70, gain).astype(BF16))
        scaled = twice_q[...] * (2.0 * gain)
        first = rounded(scaled)
        qa[:, LANES:] = jnp.where(low_lane, first, scaled - first).astype(BF16)
        gq[...] = qd[h] * high_16

        def block(qb):
            at = slice(qb * TILE, (qb + 1) * TILE)
            q_tile, g_tile = qa[at, :], gq[at, :]
            for kb in range(na):
                keys = slice(kb * rows, (kb + 1) * rows)
                s = nt_dot(ka[keys, :], q_tile)
                p = nt_dot(kv[h, keys, :], g_tile)
                top = jnp.max(jnp.max(s.reshape(rows // 8, 8, TILE), axis=0), axis=0, keepdims=True)
                e = jnp.exp(s - top)
                scores[slot, keys, at] = e
                probs[slot, keys, at] = p
                block_max[slot, kb:kb + 1, at] = top
                totals[kb, :, at] = jnp.sum(e.reshape(rows // 8, 8, TILE), axis=0)
                moments[kb, :, at] = jnp.sum((e * p).reshape(rows // 8, 8, TILE), axis=0)

        for qb in range(nq // TILE):
            block(qb)
            if qb == 2:
                @pl.when(h < last - 1)
                def _():
                    gather_forward(h + 2)

                @pl.when(h < last - 2)
                def _():
                    gather_start(h + 3)

        top = jnp.max(block_max[slot], axis=0, keepdims=True)
        share = jnp.exp(block_max[slot] - top)
        total = sum(totals[kb] * share[kb:kb + 1] for kb in range(na))
        moment = sum(moments[kb] * share[kb:kb + 1] for kb in range(na))
        total = jnp.sum(total, axis=0, keepdims=True)
        moment = jnp.sum(moment, axis=0, keepdims=True) / total
        log_sum = top + jnp.log(total)
        for row in range(nz):
            cols = slice(row * rows, (row + 1) * rows)
            stats[h, z, row:row + 1, :] = log_sum[:, cols]
            stats[h, z, row + 8:row + 9, :] = moment[:, cols]
        own = stats.at[h, z]
        spread_z(lambda other: own, own, st_send.at[h], st_recv.at[h])

    def second_pass(h, final):
        slot = h % SLOTS
        gain = gain_ref[h]
        qx[:, :LANES] = qd[h]
        ket[:64, :] = jnp.transpose(kv[h].astype(F32))[:64].astype(BF16)
        bytes_of(stats.at[h, pl.ds(0, nz - 1)], st_recv.at[h])
        top = stats[h, 0, 0:8, :]
        for other in range(1, nz):
            top = jnp.maximum(top, stats[h, other, 0:8, :])
        total = jnp.zeros((8, LANES), F32)
        moment = jnp.zeros((8, LANES), F32)
        for other in range(nz):
            share = jnp.exp(stats[h, other, 0:8, :] - top)
            total = total + share
            moment = moment + stats[h, other, 8:16, :] * share
        combined[0:8, :] = top + jnp.log(total)
        combined[8:16, :] = moment / total

        log_total = jnp.concatenate([combined[row:row + 1, :] for row in range(nz)], axis=1)
        delta_row = jnp.concatenate([combined[8 + row:9 + row, :] for row in range(nz)], axis=1)
        shares[...] = jnp.exp(block_max[slot] - log_total)

        def query_block(qb):
            at = slice(qb * TILE, (qb + 1) * TILE)
            delta = delta_row[:, at]
            for kb in range(na):
                keys = slice(kb * rows, (kb + 1) * rows)
                w = scores[slot, keys, at] * shares[kb:kb + 1, at]
                d = w * (probs[slot, keys, at] - delta)
                wd16[2 * kb * rows:(2 * kb + 1) * rows, at] = w.astype(BF16)
                wd16[(2 * kb + 1) * rows:(2 * kb + 2) * rows, at] = d.astype(BF16)
            dqt = jnp.zeros((64 + EMB_ROWS, TILE), F32)
            for kb in range(nk // TILE):
                d_tile = jnp.concatenate([
                    wd16[(2 * b + 1) * rows:(2 * b + 2) * rows, at]
                    for b in range(kb * TILE // rows, (kb + 1) * TILE // rows)], axis=0)
                dqt = dqt + nn_dot(ket[:, kb * TILE:(kb + 1) * TILE], d_tile)
            row_emb[:, at] += gain * dqt[64:, :]
            dq_out[h, :, at] = (dqt[:64, :] * 0.125).astype(BF16)

        for qb in range(nq // TILE):
            query_block(qb)
        if final:
            emb_out[0] = (-2.0 * (
                row_emb[ONE_LANE:ONE_LANE + 1, :] * eqt[:64, :] - row_emb[:64, :]
            )).astype(BF16)
            spread_z(
                lambda other: emb_out.at[0, :, pl.ds(pl.multiple_of(other * rows, rows), rows)],
                emb_in.at[0, z], em_send.at[0], em_recv.at[0])
        spread_z(
            lambda other: dq_out.at[h, :, pl.ds(pl.multiple_of(other * rows, rows), rows)],
            dq_in.at[h, z], dq_send.at[h], dq_recv.at[h])

        for kb in range(nk // TILE):
            at = kb * TILE
            both = nn_dot(wd16[2 * at:2 * (at + TILE), :], qx[...])
            for part in range(TILE // rows):
                here = slice(at + part * rows, at + (part + 1) * rows)
                grad_v = both[2 * part * rows:(2 * part + 1) * rows, :LANES]
                grad_k = both[(2 * part + 1) * rows:(2 * part + 2) * rows]
                dkv_out[h, here, :] = jnp.where(low_lane, grad_k[:, :LANES], grad_v).astype(BF16)
                col_emb[here, :] += gain * grad_k[:, LANES:]
            if final:
                here = slice(at, at + TILE)
                col_t = jnp.transpose(col_emb[here, :])
                emb_out[1, :, here] = (-2.0 * (
                    col_t[ONE_LANE:ONE_LANE + 1, :] * ek[:, here].astype(F32) - col_t[:64, :]
                )).astype(BF16)
                for part in range(TILE // rows):
                    other = kb * (TILE // rows) + part
                    here = pl.ds(at + part * rows, rows)
                    send_a(other, emb_out.at[1, :, here], emb_in.at[1, a],
                           em_send.at[1], em_recv.at[1])
                    send_a(other, dkv_out.at[h, here, :], dkv_in.at[h, a],
                           dkv_send.at[h], dkv_recv.at[h])
        if not final:
            for step in range(1, na):
                other = (a + step) % na
                pltpu.make_async_remote_copy(
                    src_ref=dkv_out.at[h, pl.ds(pl.multiple_of(other * rows, rows), rows), :],
                    dst_ref=dkv_in.at[h, a], send_sem=dkv_send.at[h], recv_sem=dkv_recv.at[h],
                    device_id=a_device(other), device_id_type=MESH).start()
        dq_in[h, z] = dq_out[h, :, pl.ds(own_q, rows)]
        dkv_in[h, a] = dkv_out[h, pl.ds(own_k, rows), :]

    def step(t, _):
        @pl.when(t < heads)
        def _():
            first_pass(t)

        @pl.when(t > 1)
        def _():
            second_pass(t - 2, False)
        return 0

    gather_end(0)
    gather_forward(1)
    lax.fori_loop(0, heads + 1, step, 0)
    second_pass(last, True)
    emb_in[0, z] = emb_out[0, :, pl.ds(own_q, rows)]
    emb_in[1, a] = emb_out[1, :, pl.ds(own_k, rows)]

    def reduce_pair(pair):
        halves = []
        for h in (2 * pair, 2 * pair + 1):
            bytes_of(dq_in.at[h, pl.ds(0, nz - 1)], dq_recv.at[h])
            bytes_of(dkv_in.at[h, pl.ds(0, na - 1)], dkv_recv.at[h])
            halves.append((
                jnp.sum(dq_in[h].astype(F32), axis=0), jnp.sum(dkv_in[h].astype(F32), axis=0)))
        cols = slice(pair * LANES, (pair + 1) * LANES)
        (q0, kv0), (q1, kv1) = halves
        dq_ref[:, cols] = jnp.transpose(jnp.concatenate([q0, q1], axis=0)).astype(BF16)
        dk_ref[:, cols] = jnp.concatenate([kv0[:, :64], kv1[:, :64]], axis=1).astype(BF16)
        dv_ref[:, cols] = jnp.concatenate([kv0[:, 64:], kv1[:, 64:]], axis=1).astype(BF16)

    def gather_sent(msg):
        whole_q, whole_k = (eq, ek) if msg is None else (qd.at[msg], kv.at[msg])
        if msg is None:
            whole_q, whole_k = eq.at[:, pl.ds(0, nq - rows)], ek.at[:, pl.ds(0, nk - rows)]
        else:
            whole_q = qd.at[msg, pl.ds(0, nq - rows), :]
            whole_k = kv.at[msg, pl.ds(0, nk - rows), :]
        bytes_of(whole_q, gz_send.at[number(msg)])
        bytes_of(whole_k, ga_send.at[number(msg)])

    for pair in range(heads // 2 - 1):
        reduce_pair(pair)
    gather_sent(None)
    for h in range(heads):
        gather_sent(h)
        bytes_of(stats.at[h, pl.ds(0, nz - 1)], st_send.at[h])
    bytes_of(emb_in.at[1, pl.ds(0, na - 1)], em_recv.at[1])
    bytes_of(emb_in.at[0, pl.ds(0, nz - 1)], em_recv.at[0])
    mine = jnp.sum(emb_in[0].astype(F32), axis=0) + jnp.sum(emb_in[1].astype(F32), axis=0)
    head_out[...] = mine
    for step in range(1, nh):
        pltpu.make_async_remote_copy(
            src_ref=head_out, dst_ref=head_in.at[head], send_sem=hd_send, recv_sem=hd_recv,
            device_id=(seq, (head + step) % nh), device_id_type=MESH).start()
    head_in[head] = mine
    reduce_pair(heads // 2 - 1)
    for h in range(heads):
        bytes_of(dq_in.at[h, pl.ds(0, nz - 1)], dq_send.at[h])
        bytes_of(dkv_in.at[h, pl.ds(0, na - 1)], dkv_send.at[h])
    bytes_of(emb_in.at[0, pl.ds(0, nz - 1)], em_send.at[0])
    bytes_of(emb_in.at[1, pl.ds(0, na - 1)], em_send.at[1])
    bytes_of(head_in.at[pl.ds(0, nh - 1)], hd_send)
    bytes_of(head_in.at[pl.ds(0, nh - 1)], hd_recv)
    de_ref[...] = jnp.sum(head_in[...], axis=0)


def hand_over(*refs):
    for source, dest in zip(refs[:4], refs[4:]):
        dest[...] = source[...]


def on_device(na, nz, nh, query_in, key_in, value_in, grad_out, embedding, bias_gain):
    rows, width = query_in.shape
    heads = width // 64
    nq, nk = nz * rows, na * rows
    vmem = pl.BlockSpec(memory_space=pltpu.VMEM)
    dma = pltpu.SemaphoreType.DMA
    grad_q, grad_k, grad_v, grad_e = pl.pallas_call(
        functools.partial(kernel, na, nz, nh),
        out_shape=(
            jax.ShapeDtypeStruct((rows, width), BF16),
            jax.ShapeDtypeStruct((rows, width), BF16),
            jax.ShapeDtypeStruct((rows, width), BF16),
            jax.ShapeDtypeStruct((64, rows), F32),
        ),
        in_specs=[pl.BlockSpec(memory_space=pltpu.SMEM)] + [pl.BlockSpec(memory_space=pl.ANY)] * 5,
        out_specs=(vmem,) * 4,
        scratch_shapes=[
            pltpu.VMEM((rows, width), BF16),
            pltpu.VMEM((rows, width), BF16),
            pltpu.VMEM((rows, width), BF16),
            pltpu.VMEM((rows, width), BF16),
            pltpu.VMEM((64, rows), BF16),
            dma((5,)),
            pltpu.VMEM((heads, nq, LANES), BF16),
            pltpu.VMEM((heads, nk, LANES), BF16),
            pltpu.VMEM((64, nq), BF16),
            pltpu.VMEM((64, nk), BF16),
            pltpu.VMEM((nk, 2 * LANES), BF16),
            pltpu.VMEM((nq, 2 * LANES), BF16),
            pltpu.VMEM((nq, LANES), BF16),
            pltpu.VMEM((nq, 2 * LANES), BF16),
            pltpu.VMEM((64 + EMB_ROWS, nk), BF16),
            pltpu.VMEM((LANES, nq), F32),
            pltpu.VMEM((nq, LANES), F32),
            pltpu.VMEM((nq, LANES), BF16),
            pltpu.VMEM((nk, LANES), BF16),
            pltpu.VMEM((SLOTS, nk, nq), F32),
            pltpu.VMEM((SLOTS, nk, nq), F32),
            pltpu.VMEM((2 * nk, nq), BF16),
            pltpu.VMEM((SLOTS, na, nq), F32),
            pltpu.VMEM((na, 8, nq), F32),
            pltpu.VMEM((na, 8, nq), F32),
            pltpu.VMEM((na, nq), F32),
            pltpu.VMEM((heads, nz, 16, LANES), F32),
            pltpu.VMEM((16, LANES), F32),
            pltpu.VMEM((EMB_ROWS, nq), F32),
            pltpu.VMEM((nk, LANES), F32),
            pltpu.VMEM((heads, 64, nq), BF16),
            pltpu.VMEM((heads, nk, LANES), BF16),
            pltpu.VMEM((heads, nz, 64, rows), BF16),
            pltpu.VMEM((heads, na, rows, LANES), BF16),
            pltpu.VMEM((2, 64, max(nq, nk)), BF16),
            pltpu.VMEM((2, max(na, nz), 64, rows), BF16),
            pltpu.VMEM((64, rows), F32),
            pltpu.VMEM((nh, 64, rows), F32),
            dma((heads + 1,)), dma((heads + 1, nz)),
            dma((heads + 1,)), dma((heads + 1, na)),
            dma((heads,)), dma((heads,)),
            dma((heads,)), dma((heads,)),
            dma((heads,)), dma((heads,)),
            dma((2,)), dma((2,)),
            dma, dma,
        ],
        compiler_params=pltpu.CompilerParams(
            collective_id=0, has_side_effects=True, vmem_limit_bytes=56 * 1024 * 1024
        ),
    )(bias_gain, query_in, key_in, value_in, grad_out, embedding.T)
    results = (grad_q, grad_k, grad_v, grad_e)
    grad_q, grad_k, grad_v, grad_e = pl.pallas_call(
        hand_over,
        out_shape=tuple(jax.ShapeDtypeStruct(r.shape, r.dtype) for r in results),
        in_specs=[vmem] * 4,
        out_specs=(vmem,) * 4,
    )(*results)
    return grad_q, grad_k, grad_v, grad_e.T


def solution(mesh):
    seq, nh = mesh.shape["seq"], mesh.shape["head"]
    nz = 1
    while nz * nz < seq:
        nz *= 2
    na = seq // nz
    placed = (
        P("seq", "head"),
        P("seq", "head"),
        P("seq", "head"),
        P("seq", "head"),
        P("seq", None),
        P("head"),
    )
    return jax.shard_map(
        functools.partial(on_device, na, nz, nh),
        mesh=mesh,
        in_specs=placed,
        out_specs=(P("seq", "head"), P("seq", "head"), P("seq", "head"), P("seq", None)),
        check_vma=False,
    )
```

```python
import functools

import jax
import jax.numpy as jnp
from jax import lax
from jax.experimental import pallas as pl
from jax.experimental.pallas import tpu as pltpu
from jax.sharding import PartitionSpec as P

MESH = pl.DeviceIdType.MESH
F32 = jnp.float32
BF16 = jnp.bfloat16
LANES = 128
TILE = 256
ONE_LANE = 76
SLOTS = 3
EMB_ROWS = 80


def nt_dot(left, right):
    return lax.dot_general(left, right, (((1,), (1,)), ((), ())), preferred_element_type=F32)


def nn_dot(left, right):
    return jnp.dot(left, right, preferred_element_type=F32)


def rounded(x):
    return x.astype(BF16).astype(F32)


def three_parts(x):
    first = rounded(x)
    second = rounded(x - first)
    return first, second, rounded(x - first - second)


def gain_pattern(base, gain):
    lane = lax.broadcasted_iota(jnp.int32, (1, LANES), 1) - base
    one, two, three = three_parts(jnp.full((1, LANES), gain, F32))
    out = jnp.where((lane == 0) | (lane == 3) | (lane == 5), -one, 0.0)
    out = jnp.where((lane == 1) | (lane == 4), -two, out)
    return jnp.where(lane == 2, -three, out)


Z_FIRST = ((0, 2, 2, 0), (0, -2, 6, 0), (0, 1, 1, 0), (0, -1, 7, 0))
Z_AHEAD = ((-2, 2, 4, 1), (-2, 1, 3, 0))
Z_BACK = ((2, -2, 0, 2), (2, -1, 5, 0))
FAR_FIRST = (4, 3, 5, 2, 6, 1, 7)


def kernel(
    na, nz, nh,
    gain_ref, q_ref, k_ref, v_ref, g_ref, emb_ref,
    dq_ref, dk_ref, dv_ref, de_ref,
    q_in, k_in, v_in, g_in, emb_in_place, in_sem,
    qbuf, kbuf, ka, qa, gq, qx, ket, eqt, twice_q, tail_q, tail_k,
    scores, probs, wd16, block_max, totals, moments, shares, stats, combined,
    row_emb, col_emb, dq_out, dkv_out, dq_in, dkv_in,
    emb_out, emb_in, head_out, head_in,
    gz_send, gz_recv, ga_send, ga_recv, st_send, st_recv,
    dq_send, dq_recv, dkv_send, dkv_recv, em_send, em_recv, hd_send, hd_recv,
):
    rows = q_ref.shape[0]
    heads = q_ref.shape[1] // 64
    nq, nk = nz * rows, na * rows
    nx = na // 2
    last = heads - 1
    seq, head = lax.axis_index("seq"), lax.axis_index("head")
    a, z = seq // nz, seq % nz
    y, x = a // nx, a % nx
    own_q = pl.multiple_of(z * rows, rows)
    own_k = pl.multiple_of(a * rows, rows)

    def z_at(step):
        return (z + step + nz) % nz

    def z_device(place):
        return (a * nz + place, head)

    def a_device(place):
        return (place * nz + z, head)

    barrier = pltpu.get_barrier_semaphore()

    def greet(target):
        pl.semaphore_signal(barrier, inc=1, device_id=target, device_id_type=MESH)

    for step in range(1, nz):
        greet(z_device(z_at(step)))
    for step in range(1, na):
        greet(a_device((a + step) % na))
    for step in range(1, nh):
        greet((seq, (head + step) % nh))

    loads = [
        pltpu.make_async_copy(source, dest, in_sem.at[i])
        for i, (source, dest) in enumerate((
            (emb_ref, emb_in_place), (q_ref, q_in), (g_ref, g_in), (k_ref, k_in), (v_ref, v_in)))
    ]
    for load in loads:
        load.start()

    def head_rows(h):
        return pl.ds(pl.multiple_of(64 + h * rows, 64), rows)

    def packed(left, right, h, scale):
        cols = slice(h * 64, (h + 1) * 64)
        return jnp.concatenate(
            [left[:, cols].astype(F32) * scale, right[:, cols].astype(F32)], axis=1).astype(BF16)

    def pack_head(h):
        qbuf[z, head_rows(h), :] = packed(q_in, g_in, h, 0.125)
        kbuf[a, head_rows(h), :] = packed(k_in, v_in, h, 1.0)

    for load in loads:
        load.wait()
    qbuf[z, 0:64, :] = emb_in_place[...]
    kbuf[a, 0:64, :] = emb_in_place[...]
    pack_head(0)

    pl.semaphore_wait(barrier, (nz - 1) + (na - 1) + (nh - 1))

    def piece(msg, buffer, place, part):
        if isinstance(msg, int) and msg == 0:
            first, size = 0, 64 + rows
        else:
            first, size = pl.multiple_of(64 + msg * rows, 64), rows
        if part:
            size = size // 2
            first = first + (size if part == 2 else 0)
        return buffer.at[place, pl.ds(first, size), :]

    def z_send(msg, plan):
        for held, to, slot, part in plan:
            block = piece(msg, qbuf, z_at(held), part)
            pltpu.make_async_remote_copy(
                src_ref=block, dst_ref=block,
                send_sem=gz_send.at[msg], recv_sem=gz_recv.at[msg, slot],
                device_id=z_device(z_at(to)), device_id_type=MESH).start()

    def z_wait(msg, slot):
        block = piece(msg, qbuf, z_at(-4 if slot == 0 else -slot), {0: 2, 4: 1}.get(slot, 0))
        pltpu.make_async_copy(block, block, gz_recv.at[msg, slot]).wait()

    def a_send(msg, partner):
        held = ((y + partner) % 2) * nx + x
        block = piece(msg, kbuf, held, 0)
        targets = [] if partner else [(4, ((y + 1) % 2) * nx + x)]
        targets += [(4 * partner + step, y * nx + (x + step) % nx) for step in (2, 1, 3)]
        for slot, place in targets:
            pltpu.make_async_remote_copy(
                src_ref=block, dst_ref=block,
                send_sem=ga_send.at[msg], recv_sem=ga_recv.at[msg, slot],
                device_id=a_device(place), device_id_type=MESH).start()

    def a_wait(msg, slot):
        held = ((y + slot // 4) % 2) * nx + (x - slot % 4 + nx) % nx
        block = piece(msg, kbuf, held, 0)
        pltpu.make_async_copy(block, block, ga_recv.at[msg, slot]).wait()

    def gather_start(msg):
        z_send(msg, Z_FIRST[:2])
        a_send(msg, 0)
        z_send(msg, Z_FIRST[2:])

    def gather_forward(msg):
        a_wait(msg, 4)
        a_send(msg, 1)
        z_wait(msg, 2)
        z_send(msg, Z_AHEAD)
        z_wait(msg, 6)
        z_send(msg, Z_BACK)

    def gather_end(msg):
        for slot in (1, 7, 3, 5, 4, 0):
            z_wait(msg, slot)
        for slot in (1, 3, 2, 5, 7, 6):
            a_wait(msg, slot)

    def spread_z(source, dest, send_sem, recv_sem):
        for step in FAR_FIRST:
            other = z_at(step)
            pltpu.make_async_remote_copy(
                src_ref=source(other), dst_ref=dest, send_sem=send_sem, recv_sem=recv_sem,
                device_id=z_device(other), device_id_type=MESH).start()

    def send_a(other, source, dest, send_sem, recv_sem):
        @pl.when(other != a)
        def _():
            pltpu.make_async_remote_copy(
                src_ref=source, dst_ref=dest, send_sem=send_sem, recv_sem=recv_sem,
                device_id=a_device(other), device_id_type=MESH).start()

    def bytes_of(block, sem):
        pltpu.make_async_copy(block, block, sem).wait()

    gather_start(0)
    pack_head(1)
    gather_start(1)
    for h in range(2, heads):
        pack_head(h)
    row_emb[...] = jnp.zeros_like(row_emb)
    col_emb[...] = jnp.zeros_like(col_emb)
    gather_forward(0)
    gather_start(2)
    gather_forward(1)
    gather_start(3)
    gather_end(0)

    def of_queries(h):
        return qbuf[:, head_rows(h), :].reshape(nq, LANES)

    def of_keys(h):
        return kbuf[:, head_rows(h), :].reshape(nk, LANES)

    def widened(emb_t, base):
        e = emb_t.astype(F32)
        one, two, three = three_parts(jnp.sum(e * e, axis=0, keepdims=True))
        row = lax.broadcasted_iota(jnp.int32, (16, e.shape[1]), 0) + (64 - base)
        extra = jnp.where((row >= 0) & (row < 3), one, 0.0)
        extra = jnp.where((row >= 3) & (row < 5), two, extra)
        extra = jnp.where(row == 5, three, extra)
        extra = jnp.where(row == ONE_LANE - base, 1.0, extra)
        return jnp.concatenate([e, extra, jnp.zeros((48, e.shape[1]), F32)], axis=0)

    low_lane = lax.broadcasted_iota(jnp.int32, (1, LANES), 1) < 64
    low_f32 = jnp.where(low_lane, 1.0, 0.0)
    high_f32 = 1.0 - low_f32
    low_16, high_16 = low_f32.astype(BF16), high_f32.astype(BF16)
    one_lane = jnp.where(lax.broadcasted_iota(jnp.int32, (1, LANES), 1) == ONE_LANE, 1.0, 0.0)

    eqt[...] = widened(jnp.concatenate([qbuf[i, 0:64, :] for i in range(nz)], axis=1), 64)
    wide_k = widened(jnp.concatenate([kbuf[i, 0:64, :] for i in range(na)], axis=1), 70)
    ket[64:, :] = wide_k[:EMB_ROWS].astype(BF16)
    wide_q = jnp.transpose(eqt[...])
    wide_k = jnp.transpose(wide_k)
    qx[:, LANES:] = wide_q.astype(BF16)
    tail_q[...] = (wide_q * high_f32).astype(BF16)
    tail_k[...] = ((wide_k - one_lane) * high_f32).astype(BF16)
    wide_q, wide_k = wide_q * low_f32, wide_k * low_f32
    twice_q[...] = wide_q + pltpu.roll(wide_q, 64, 1)
    ka[:, LANES:] = (wide_k + pltpu.roll(wide_k, 64, 1)).astype(BF16)

    def first_pass(h):
        slot = h % SLOTS
        @pl.when(h > 0)
        def _():
            gather_end(h)

        gain = gain_ref[h]
        ka[:, :LANES] = of_keys(h) * low_16 + (tail_k[...] + gain_pattern(64, gain).astype(BF16))
        qa[:, :LANES] = of_queries(h) * low_16 + (tail_q[...] + gain_pattern(70, gain).astype(BF16))
        scaled = twice_q[...] * (2.0 * gain)
        first = rounded(scaled)
        qa[:, LANES:] = jnp.where(low_lane, first, scaled - first).astype(BF16)
        gq[...] = of_queries(h) * high_16

        def block(qb):
            at = slice(qb * TILE, (qb + 1) * TILE)
            q_tile, g_tile = qa[at, :], gq[at, :]
            for kb in range(na):
                keys = slice(kb * rows, (kb + 1) * rows)
                s = nt_dot(ka[keys, :], q_tile)
                p = nt_dot(kbuf[kb, head_rows(h), :], g_tile)
                top = jnp.max(jnp.max(s.reshape(rows // 8, 8, TILE), axis=0), axis=0, keepdims=True)
                e = jnp.exp(s - top)
                scores[slot, keys, at] = e
                probs[slot, keys, at] = p
                block_max[slot, kb:kb + 1, at] = top
                totals[kb, :, at] = jnp.sum(e.reshape(rows // 8, 8, TILE), axis=0)
                moments[kb, :, at] = jnp.sum((e * p).reshape(rows // 8, 8, TILE), axis=0)

        for qb in range(nq // TILE):
            block(qb)
            if qb == 1:
                @pl.when(h < last - 1)
                def _():
                    gather_forward(h + 2)

        top = jnp.max(block_max[slot], axis=0, keepdims=True)
        share = jnp.exp(block_max[slot] - top)
        total = sum(totals[kb] * share[kb:kb + 1] for kb in range(na))
        moment = sum(moments[kb] * share[kb:kb + 1] for kb in range(na))
        total = jnp.sum(total, axis=0, keepdims=True)
        moment = jnp.sum(moment, axis=0, keepdims=True) / total
        log_sum = top + jnp.log(total)
        for row in range(nz):
            cols = slice(row * rows, (row + 1) * rows)
            stats[h, z, row:row + 1, :] = log_sum[:, cols]
            stats[h, z, row + 8:row + 9, :] = moment[:, cols]
        own = stats.at[h, z]
        spread_z(lambda other: own, own, st_send.at[h], st_recv.at[h])

    def second_pass(h, final):
        slot = h % SLOTS
        gain = gain_ref[h]
        qx[:, :LANES] = of_queries(h)
        ket[:64, :] = jnp.transpose(of_keys(h).astype(F32))[:64].astype(BF16)
        bytes_of(stats.at[h, pl.ds(0, nz - 1)], st_recv.at[h])
        top = stats[h, 0, 0:8, :]
        for other in range(1, nz):
            top = jnp.maximum(top, stats[h, other, 0:8, :])
        total = jnp.zeros((8, LANES), F32)
        moment = jnp.zeros((8, LANES), F32)
        for other in range(nz):
            share = jnp.exp(stats[h, other, 0:8, :] - top)
            total = total + share
            moment = moment + stats[h, other, 8:16, :] * share
        combined[0:8, :] = top + jnp.log(total)
        combined[8:16, :] = moment / total

        log_total = jnp.concatenate([combined[row:row + 1, :] for row in range(nz)], axis=1)
        delta_row = jnp.concatenate([combined[8 + row:9 + row, :] for row in range(nz)], axis=1)
        shares[...] = jnp.exp(block_max[slot] - log_total)

        def query_block(qb):
            at = slice(qb * TILE, (qb + 1) * TILE)
            delta = delta_row[:, at]
            for kb in range(na):
                keys = slice(kb * rows, (kb + 1) * rows)
                w = scores[slot, keys, at] * shares[kb:kb + 1, at]
                d = w * (probs[slot, keys, at] - delta)
                wd16[2 * kb * rows:(2 * kb + 1) * rows, at] = w.astype(BF16)
                wd16[(2 * kb + 1) * rows:(2 * kb + 2) * rows, at] = d.astype(BF16)
            dqt = jnp.zeros((64 + EMB_ROWS, TILE), F32)
            for kb in range(nk // TILE):
                d_tile = jnp.concatenate([
                    wd16[(2 * b + 1) * rows:(2 * b + 2) * rows, at]
                    for b in range(kb * TILE // rows, (kb + 1) * TILE // rows)], axis=0)
                dqt = dqt + nn_dot(ket[:, kb * TILE:(kb + 1) * TILE], d_tile)
            row_emb[:, at] += gain * dqt[64:, :]
            dq_out[h, :, at] = (dqt[:64, :] * 0.125).astype(BF16)

        for qb in range(nq // TILE):
            query_block(qb)
        if final:
            emb_out[0] = (-2.0 * (
                row_emb[ONE_LANE:ONE_LANE + 1, :] * eqt[:64, :] - row_emb[:64, :]
            )).astype(BF16)
            spread_z(
                lambda other: emb_out.at[0, :, pl.ds(pl.multiple_of(other * rows, rows), rows)],
                emb_in.at[0, z], em_send.at[0], em_recv.at[0])
        spread_z(
            lambda other: dq_out.at[h, :, pl.ds(pl.multiple_of(other * rows, rows), rows)],
            dq_in.at[h, z], dq_send.at[h], dq_recv.at[h])

        for kb in range(nk // TILE):
            at = kb * TILE
            both = nn_dot(wd16[2 * at:2 * (at + TILE), :], qx[...])
            for part in range(TILE // rows):
                here = slice(at + part * rows, at + (part + 1) * rows)
                grad_v = both[2 * part * rows:(2 * part + 1) * rows, :LANES]
                grad_k = both[(2 * part + 1) * rows:(2 * part + 2) * rows]
                dkv_out[h, here, :] = jnp.where(low_lane, grad_k[:, :LANES], grad_v).astype(BF16)
                col_emb[here, :] += gain * grad_k[:, LANES:]
            if final:
                here = slice(at, at + TILE)
                col_t = jnp.transpose(col_emb[here, :])
                emb_out[1, :, here] = (-2.0 * (
                    col_t[ONE_LANE:ONE_LANE + 1, :] * ket[64:128, here].astype(F32) - col_t[:64, :]
                )).astype(BF16)
                for part in range(TILE // rows):
                    other = kb * (TILE // rows) + part
                    here = pl.ds(at + part * rows, rows)
                    send_a(other, emb_out.at[1, :, here], emb_in.at[1, a],
                           em_send.at[1], em_recv.at[1])
                    send_a(other, dkv_out.at[h, here, :], dkv_in.at[h, a],
                           dkv_send.at[h], dkv_recv.at[h])
        if not final:
            for step in range(1, na):
                other = (a + step) % na
                pltpu.make_async_remote_copy(
                    src_ref=dkv_out.at[h, pl.ds(pl.multiple_of(other * rows, rows), rows), :],
                    dst_ref=dkv_in.at[h, a], send_sem=dkv_send.at[h], recv_sem=dkv_recv.at[h],
                    device_id=a_device(other), device_id_type=MESH).start()
        dq_in[h, z] = dq_out[h, :, pl.ds(own_q, rows)]
        dkv_in[h, a] = dkv_out[h, pl.ds(own_k, rows), :]

    def step(t, _):
        @pl.when(t < heads)
        def _():
            first_pass(t)

        @pl.when(t > 1)
        def _():
            second_pass(t - 2, False)
        return 0

    lax.fori_loop(0, heads + 1, step, 0)
    second_pass(last, True)
    emb_in[0, z] = emb_out[0, :, pl.ds(own_q, rows)]
    emb_in[1, a] = emb_out[1, :, pl.ds(own_k, rows)]

    def reduce_pair(pair):
        halves = []
        for h in (2 * pair, 2 * pair + 1):
            bytes_of(dq_in.at[h, pl.ds(0, nz - 1)], dq_recv.at[h])
            bytes_of(dkv_in.at[h, pl.ds(0, na - 1)], dkv_recv.at[h])
            halves.append((
                jnp.sum(dq_in[h].astype(F32), axis=0), jnp.sum(dkv_in[h].astype(F32), axis=0)))
        cols = slice(pair * LANES, (pair + 1) * LANES)
        (q0, kv0), (q1, kv1) = halves
        dq_ref[:, cols] = jnp.transpose(jnp.concatenate([q0, q1], axis=0)).astype(BF16)
        dk_ref[:, cols] = jnp.concatenate([kv0[:, :64], kv1[:, :64]], axis=1).astype(BF16)
        dv_ref[:, cols] = jnp.concatenate([kv0[:, 64:], kv1[:, 64:]], axis=1).astype(BF16)

    def gather_sent(msg):
        first, size = (64 + msg * rows, rows) if msg else (0, 64 + rows)
        bytes_of(qbuf.at[pl.ds(0, nz - 1), pl.ds(first, size), :], gz_send.at[msg])
        bytes_of(kbuf.at[pl.ds(0, na - 1), pl.ds(first, size), :], ga_send.at[msg])

    for pair in range(heads // 2 - 1):
        reduce_pair(pair)
    for h in range(heads):
        gather_sent(h)
        bytes_of(stats.at[h, pl.ds(0, nz - 1)], st_send.at[h])
    bytes_of(emb_in.at[1, pl.ds(0, na - 1)], em_recv.at[1])
    bytes_of(emb_in.at[0, pl.ds(0, nz - 1)], em_recv.at[0])
    mine = jnp.sum(emb_in[0].astype(F32), axis=0) + jnp.sum(emb_in[1].astype(F32), axis=0)
    mine = mine.astype(BF16)
    head_out[...] = mine
    for step in range(1, nh):
        pltpu.make_async_remote_copy(
            src_ref=head_out, dst_ref=head_in.at[head], send_sem=hd_send, recv_sem=hd_recv,
            device_id=(seq, (head + step) % nh), device_id_type=MESH).start()
    head_in[head] = mine
    reduce_pair(heads // 2 - 1)
    for h in range(heads):
        bytes_of(dq_in.at[h, pl.ds(0, nz - 1)], dq_send.at[h])
        bytes_of(dkv_in.at[h, pl.ds(0, na - 1)], dkv_send.at[h])
    bytes_of(emb_in.at[0, pl.ds(0, nz - 1)], em_send.at[0])
    bytes_of(emb_in.at[1, pl.ds(0, na - 1)], em_send.at[1])
    bytes_of(head_in.at[pl.ds(0, nh - 1)], hd_send)
    bytes_of(head_in.at[pl.ds(0, nh - 1)], hd_recv)
    de_ref[...] = jnp.sum(head_in[...].astype(F32), axis=0)


def hand_over(*refs):
    for source, dest in zip(refs[:4], refs[4:]):
        dest[...] = source[...]


def on_device(na, nz, nh, query_in, key_in, value_in, grad_out, embedding, bias_gain):
    rows, width = query_in.shape
    heads = width // 64
    nq, nk = nz * rows, na * rows
    vmem = pl.BlockSpec(memory_space=pltpu.VMEM)
    dma = pltpu.SemaphoreType.DMA
    grad_q, grad_k, grad_v, grad_e = pl.pallas_call(
        functools.partial(kernel, na, nz, nh),
        out_shape=(
            jax.ShapeDtypeStruct((rows, width), BF16),
            jax.ShapeDtypeStruct((rows, width), BF16),
            jax.ShapeDtypeStruct((rows, width), BF16),
            jax.ShapeDtypeStruct((64, rows), F32),
        ),
        in_specs=[pl.BlockSpec(memory_space=pltpu.SMEM)] + [pl.BlockSpec(memory_space=pl.ANY)] * 5,
        out_specs=(vmem,) * 4,
        scratch_shapes=[
            pltpu.VMEM((rows, width), BF16),
            pltpu.VMEM((rows, width), BF16),
            pltpu.VMEM((rows, width), BF16),
            pltpu.VMEM((rows, width), BF16),
            pltpu.VMEM((64, rows), BF16),
            dma((5,)),
            pltpu.VMEM((nz, 64 + heads * rows, LANES), BF16),
            pltpu.VMEM((na, 64 + heads * rows, LANES), BF16),
            pltpu.VMEM((nk, 2 * LANES), BF16),
            pltpu.VMEM((nq, 2 * LANES), BF16),
            pltpu.VMEM((nq, LANES), BF16),
            pltpu.VMEM((nq, 2 * LANES), BF16),
            pltpu.VMEM((64 + EMB_ROWS, nk), BF16),
            pltpu.VMEM((LANES, nq), F32),
            pltpu.VMEM((nq, LANES), F32),
            pltpu.VMEM((nq, LANES), BF16),
            pltpu.VMEM((nk, LANES), BF16),
            pltpu.VMEM((SLOTS, nk, nq), F32),
            pltpu.VMEM((SLOTS, nk, nq), F32),
            pltpu.VMEM((2 * nk, nq), BF16),
            pltpu.VMEM((SLOTS, na, nq), F32),
            pltpu.VMEM((na, 8, nq), F32),
            pltpu.VMEM((na, 8, nq), F32),
            pltpu.VMEM((na, nq), F32),
            pltpu.VMEM((heads, nz, 16, LANES), F32),
            pltpu.VMEM((16, LANES), F32),
            pltpu.VMEM((EMB_ROWS, nq), F32),
            pltpu.VMEM((nk, LANES), F32),
            pltpu.VMEM((heads, 64, nq), BF16),
            pltpu.VMEM((heads, nk, LANES), BF16),
            pltpu.VMEM((heads, nz, 64, rows), BF16),
            pltpu.VMEM((heads, na, rows, LANES), BF16),
            pltpu.VMEM((2, 64, max(nq, nk)), BF16),
            pltpu.VMEM((2, max(na, nz), 64, rows), BF16),
            pltpu.VMEM((64, rows), BF16),
            pltpu.VMEM((nh, 64, rows), BF16),
            dma((heads,)), dma((heads, nz)),
            dma((heads,)), dma((heads, na)),
            dma((heads,)), dma((heads,)),
            dma((heads,)), dma((heads,)),
            dma((heads,)), dma((heads,)),
            dma((2,)), dma((2,)),
            dma, dma,
        ],
        compiler_params=pltpu.CompilerParams(
            collective_id=0, has_side_effects=True, vmem_limit_bytes=56 * 1024 * 1024
        ),
    )(bias_gain, query_in, key_in, value_in, grad_out, embedding.T)
    results = (grad_q, grad_k, grad_v, grad_e)
    grad_q, grad_k, grad_v, grad_e = pl.pallas_call(
        hand_over,
        out_shape=tuple(jax.ShapeDtypeStruct(r.shape, r.dtype) for r in results),
        in_specs=[vmem] * 4,
        out_specs=(vmem,) * 4,
    )(*results)
    return grad_q, grad_k, grad_v, grad_e.T


def solution(mesh):
    seq, nh = mesh.shape["seq"], mesh.shape["head"]
    nz = 1
    while nz * nz < seq:
        nz *= 2
    na = seq // nz
    placed = (
        P("seq", "head"),
        P("seq", "head"),
        P("seq", "head"),
        P("seq", "head"),
        P("seq", None),
        P("head"),
    )
    return jax.shard_map(
        functools.partial(on_device, na, nz, nh),
        mesh=mesh,
        in_specs=placed,
        out_specs=(P("seq", "head"), P("seq", "head"), P("seq", "head"), P("seq", None)),
        check_vma=False,
    )
```

```python
import functools

import jax
import jax.numpy as jnp
from jax import lax
from jax.experimental import pallas as pl
from jax.experimental.pallas import tpu as pltpu
from jax.sharding import PartitionSpec as P

MESH = pl.DeviceIdType.MESH
F32 = jnp.float32
BF16 = jnp.bfloat16
LANES = 128
TILE = 256
ONE_LANE = 76
SLOTS = 3
EMB_ROWS = 80


def nt_dot(left, right):
    return lax.dot_general(left, right, (((1,), (1,)), ((), ())), preferred_element_type=F32)


def nn_dot(left, right):
    return jnp.dot(left, right, preferred_element_type=F32)


def rounded(x):
    return x.astype(BF16).astype(F32)


def three_parts(x):
    first = rounded(x)
    second = rounded(x - first)
    return first, second, rounded(x - first - second)


def gain_pattern(base, gain):
    lane = lax.broadcasted_iota(jnp.int32, (1, LANES), 1) - base
    one, two, three = three_parts(jnp.full((1, LANES), gain, F32))
    out = jnp.where((lane == 0) | (lane == 3) | (lane == 5), -one, 0.0)
    out = jnp.where((lane == 1) | (lane == 4), -two, out)
    return jnp.where(lane == 2, -three, out)


Z_FIRST = ((0, 2, 2, 0), (0, -2, 6, 0), (0, 1, 1, 0), (0, -1, 7, 0))
Z_AHEAD = ((-2, 2, 4, 1), (-2, 1, 3, 0))
Z_BACK = ((2, -2, 0, 2), (2, -1, 5, 0))
FAR_FIRST = (4, 3, 5, 2, 6, 1, 7)


def kernel(
    na, nz, nh,
    gain_ref, q_ref, k_ref, v_ref, g_ref, emb_ref,
    dq_ref, dk_ref, dv_ref, de_ref,
    q_in, k_in, v_in, g_in, emb_in_place, in_sem, total_emb, out_sem,
    qbuf, kbuf, ka, qa, gq, qx, ket, eqt, twice_q, tail_q, tail_k,
    scores, probs, wd16, block_max, totals, moments, shares, stats, combined,
    row_emb, col_emb, dq_out, dkv_out, dq_in, dkv_in,
    emb_out, emb_in, head_out, head_in,
    gz_send, gz_recv, ga_send, ga_recv, st_send, st_recv,
    dq_send, dq_recv, dkv_send, dkv_recv, em_send, em_recv, hd_send, hd_recv,
):
    rows = q_ref.shape[0]
    heads = q_ref.shape[1] // 64
    nq, nk = nz * rows, na * rows
    nx = na // 2
    last = heads - 1
    seq, head = lax.axis_index("seq"), lax.axis_index("head")
    a, z = seq // nz, seq % nz
    y, x = a // nx, a % nx
    own_q = pl.multiple_of(z * rows, rows)
    own_k = pl.multiple_of(a * rows, rows)

    def z_at(step):
        return (z + step + nz) % nz

    def z_device(place):
        return (a * nz + place, head)

    def a_device(place):
        return (place * nz + z, head)

    barrier = pltpu.get_barrier_semaphore()

    def greet(target):
        pl.semaphore_signal(barrier, inc=1, device_id=target, device_id_type=MESH)

    for step in range(1, nz):
        greet(z_device(z_at(step)))
    for step in range(1, na):
        greet(a_device((a + step) % na))
    for step in range(1, nh):
        greet((seq, (head + step) % nh))

    loads = [
        pltpu.make_async_copy(source, dest, in_sem.at[i])
        for i, (source, dest) in enumerate((
            (emb_ref, emb_in_place), (q_ref, q_in), (g_ref, g_in), (k_ref, k_in), (v_ref, v_in)))
    ]
    for load in loads:
        load.start()

    def head_rows(h):
        return pl.ds(pl.multiple_of(64 + h * rows, 64), rows)

    def packed(left, right, h, scale):
        cols = slice(h * 64, (h + 1) * 64)
        return jnp.concatenate(
            [left[:, cols].astype(F32) * scale, right[:, cols].astype(F32)], axis=1).astype(BF16)

    def pack_head(h):
        qbuf[z, head_rows(h), :] = packed(q_in, g_in, h, 0.125)
        kbuf[a, head_rows(h), :] = packed(k_in, v_in, h, 1.0)

    for load in loads:
        load.wait()
    qbuf[z, 0:64, :] = emb_in_place[...]
    kbuf[a, 0:64, :] = emb_in_place[...]
    pack_head(0)

    pl.semaphore_wait(barrier, (nz - 1) + (na - 1) + (nh - 1))

    def piece(msg, buffer, place, part):
        if isinstance(msg, int) and msg == 0:
            first, size = 0, 64 + rows
        else:
            first, size = pl.multiple_of(64 + msg * rows, 64), rows
        if part:
            size = size // 2
            first = first + (size if part == 2 else 0)
        return buffer.at[place, pl.ds(first, size), :]

    def z_send(msg, plan):
        for held, to, slot, part in plan:
            block = piece(msg, qbuf, z_at(held), part)
            pltpu.make_async_remote_copy(
                src_ref=block, dst_ref=block,
                send_sem=gz_send.at[msg], recv_sem=gz_recv.at[msg, slot],
                device_id=z_device(z_at(to)), device_id_type=MESH).start()

    def z_wait(msg, slot):
        block = piece(msg, qbuf, z_at(-4 if slot == 0 else -slot), {0: 2, 4: 1}.get(slot, 0))
        pltpu.make_async_copy(block, block, gz_recv.at[msg, slot]).wait()

    def a_send(msg, partner):
        held = ((y + partner) % 2) * nx + x
        block = piece(msg, kbuf, held, 0)
        targets = [] if partner else [(4, ((y + 1) % 2) * nx + x)]
        targets += [(4 * partner + step, y * nx + (x + step) % nx) for step in (2, 1, 3)]
        for slot, place in targets:
            pltpu.make_async_remote_copy(
                src_ref=block, dst_ref=block,
                send_sem=ga_send.at[msg], recv_sem=ga_recv.at[msg, slot],
                device_id=a_device(place), device_id_type=MESH).start()

    def a_wait(msg, slot):
        held = ((y + slot // 4) % 2) * nx + (x - slot % 4 + nx) % nx
        block = piece(msg, kbuf, held, 0)
        pltpu.make_async_copy(block, block, ga_recv.at[msg, slot]).wait()

    def gather_start(msg):
        z_send(msg, Z_FIRST[:2])
        a_send(msg, 0)
        z_send(msg, Z_FIRST[2:])

    def gather_forward(msg):
        a_wait(msg, 4)
        a_send(msg, 1)
        z_wait(msg, 2)
        z_send(msg, Z_AHEAD)
        z_wait(msg, 6)
        z_send(msg, Z_BACK)

    def gather_end(msg):
        for slot in (1, 7, 3, 5, 4, 0):
            z_wait(msg, slot)
        for slot in (1, 3, 2, 5, 7, 6):
            a_wait(msg, slot)

    def spread_z(source, dest, send_sem, recv_sem):
        for step in FAR_FIRST:
            other = z_at(step)
            pltpu.make_async_remote_copy(
                src_ref=source(other), dst_ref=dest, send_sem=send_sem, recv_sem=recv_sem,
                device_id=z_device(other), device_id_type=MESH).start()

    def send_a(other, source, dest, send_sem, recv_sem):
        @pl.when(other != a)
        def _():
            pltpu.make_async_remote_copy(
                src_ref=source, dst_ref=dest, send_sem=send_sem, recv_sem=recv_sem,
                device_id=a_device(other), device_id_type=MESH).start()

    def bytes_of(block, sem):
        pltpu.make_async_copy(block, block, sem).wait()

    gather_start(0)
    pack_head(1)
    gather_start(1)
    for h in range(2, heads):
        pack_head(h)
    row_emb[...] = jnp.zeros_like(row_emb)
    col_emb[...] = jnp.zeros_like(col_emb)
    gather_forward(0)
    gather_start(2)
    gather_forward(1)
    gather_start(3)
    gather_end(0)

    def of_queries(h):
        return qbuf[:, head_rows(h), :].reshape(nq, LANES)

    def of_keys(h):
        return kbuf[:, head_rows(h), :].reshape(nk, LANES)

    def widened(emb_t, base):
        e = emb_t.astype(F32)
        one, two, three = three_parts(jnp.sum(e * e, axis=0, keepdims=True))
        row = lax.broadcasted_iota(jnp.int32, (16, e.shape[1]), 0) + (64 - base)
        extra = jnp.where((row >= 0) & (row < 3), one, 0.0)
        extra = jnp.where((row >= 3) & (row < 5), two, extra)
        extra = jnp.where(row == 5, three, extra)
        extra = jnp.where(row == ONE_LANE - base, 1.0, extra)
        return jnp.concatenate([e, extra, jnp.zeros((48, e.shape[1]), F32)], axis=0)

    low_lane = lax.broadcasted_iota(jnp.int32, (1, LANES), 1) < 64
    low_f32 = jnp.where(low_lane, 1.0, 0.0)
    high_f32 = 1.0 - low_f32
    low_16, high_16 = low_f32.astype(BF16), high_f32.astype(BF16)
    one_lane = jnp.where(lax.broadcasted_iota(jnp.int32, (1, LANES), 1) == ONE_LANE, 1.0, 0.0)

    eqt[...] = widened(jnp.concatenate([qbuf[i, 0:64, :] for i in range(nz)], axis=1), 64)
    wide_k = widened(jnp.concatenate([kbuf[i, 0:64, :] for i in range(na)], axis=1), 70)
    ket[64:, :] = wide_k[:EMB_ROWS].astype(BF16)
    wide_q = jnp.transpose(eqt[...])
    wide_k = jnp.transpose(wide_k)
    qx[:, LANES:] = wide_q.astype(BF16)
    tail_q[...] = (wide_q * high_f32).astype(BF16)
    tail_k[...] = ((wide_k - one_lane) * high_f32).astype(BF16)
    wide_q, wide_k = wide_q * low_f32, wide_k * low_f32
    twice_q[...] = wide_q + pltpu.roll(wide_q, 64, 1)
    ka[:, LANES:] = (wide_k + pltpu.roll(wide_k, 64, 1)).astype(BF16)

    def first_pass(h):
        slot = h % SLOTS
        @pl.when(h > 0)
        def _():
            gather_end(h)

        gain = gain_ref[h]
        ka[:, :LANES] = of_keys(h) * low_16 + (tail_k[...] + gain_pattern(64, gain).astype(BF16))
        qa[:, :LANES] = of_queries(h) * low_16 + (tail_q[...] + gain_pattern(70, gain).astype(BF16))
        scaled = twice_q[...] * (2.0 * gain)
        first = rounded(scaled)
        qa[:, LANES:] = jnp.where(low_lane, first, scaled - first).astype(BF16)
        gq[...] = of_queries(h) * high_16

        def block(qb):
            at = slice(qb * TILE, (qb + 1) * TILE)
            q_tile, g_tile = qa[at, :], gq[at, :]
            for kb in range(na):
                keys = slice(kb * rows, (kb + 1) * rows)
                s = nt_dot(ka[keys, :], q_tile)
                p = nt_dot(kbuf[kb, head_rows(h), :], g_tile)
                top = jnp.max(jnp.max(s.reshape(rows // 8, 8, TILE), axis=0), axis=0, keepdims=True)
                e = jnp.exp(s - top)
                scores[slot, keys, at] = e
                probs[slot, keys, at] = p
                block_max[slot, kb:kb + 1, at] = top
                totals[kb, :, at] = jnp.sum(e.reshape(rows // 8, 8, TILE), axis=0)
                moments[kb, :, at] = jnp.sum((e * p).reshape(rows // 8, 8, TILE), axis=0)

        for qb in range(nq // TILE):
            block(qb)
            if qb == 1:
                @pl.when(h < last - 1)
                def _():
                    gather_forward(h + 2)

        top = jnp.max(block_max[slot], axis=0, keepdims=True)
        share = jnp.exp(block_max[slot] - top)
        total = sum(totals[kb] * share[kb:kb + 1] for kb in range(na))
        moment = sum(moments[kb] * share[kb:kb + 1] for kb in range(na))
        total = jnp.sum(total, axis=0, keepdims=True)
        moment = jnp.sum(moment, axis=0, keepdims=True) / total
        log_sum = top + jnp.log(total)
        for row in range(nz):
            cols = slice(row * rows, (row + 1) * rows)
            stats[h, z, row:row + 1, :] = log_sum[:, cols]
            stats[h, z, row + 8:row + 9, :] = moment[:, cols]
        own = stats.at[h, z]
        spread_z(lambda other: own, own, st_send.at[h], st_recv.at[h])

    def second_pass(h, final):
        slot = h % SLOTS
        gain = gain_ref[h]
        qx[:, :LANES] = of_queries(h)
        ket[:64, :] = jnp.transpose(of_keys(h).astype(F32))[:64].astype(BF16)
        bytes_of(stats.at[h, pl.ds(0, nz - 1)], st_recv.at[h])
        top = stats[h, 0, 0:8, :]
        for other in range(1, nz):
            top = jnp.maximum(top, stats[h, other, 0:8, :])
        total = jnp.zeros((8, LANES), F32)
        moment = jnp.zeros((8, LANES), F32)
        for other in range(nz):
            share = jnp.exp(stats[h, other, 0:8, :] - top)
            total = total + share
            moment = moment + stats[h, other, 8:16, :] * share
        combined[0:8, :] = top + jnp.log(total)
        combined[8:16, :] = moment / total

        log_total = jnp.concatenate([combined[row:row + 1, :] for row in range(nz)], axis=1)
        delta_row = jnp.concatenate([combined[8 + row:9 + row, :] for row in range(nz)], axis=1)
        shares[...] = jnp.exp(block_max[slot] - log_total)

        def query_block(qb):
            at = slice(qb * TILE, (qb + 1) * TILE)
            delta = delta_row[:, at]
            for kb in range(na):
                keys = slice(kb * rows, (kb + 1) * rows)
                w = scores[slot, keys, at] * shares[kb:kb + 1, at]
                d = w * (probs[slot, keys, at] - delta)
                wd16[2 * kb * rows:(2 * kb + 1) * rows, at] = w.astype(BF16)
                wd16[(2 * kb + 1) * rows:(2 * kb + 2) * rows, at] = d.astype(BF16)
            dqt = jnp.zeros((64 + EMB_ROWS, TILE), F32)
            for kb in range(nk // TILE):
                d_tile = jnp.concatenate([
                    wd16[(2 * b + 1) * rows:(2 * b + 2) * rows, at]
                    for b in range(kb * TILE // rows, (kb + 1) * TILE // rows)], axis=0)
                dqt = dqt + nn_dot(ket[:, kb * TILE:(kb + 1) * TILE], d_tile)
            row_emb[:, at] += gain * dqt[64:, :]
            dq_out[h, :, at] = (dqt[:64, :] * 0.125).astype(BF16)

        for qb in range(nq // TILE):
            query_block(qb)
        if final:
            emb_out[0] = (-2.0 * (
                row_emb[ONE_LANE:ONE_LANE + 1, :] * eqt[:64, :] - row_emb[:64, :]
            )).astype(BF16)
            spread_z(
                lambda other: emb_out.at[0, :, pl.ds(pl.multiple_of(other * rows, rows), rows)],
                emb_in.at[0, z], em_send.at[0], em_recv.at[0])
        spread_z(
            lambda other: dq_out.at[h, :, pl.ds(pl.multiple_of(other * rows, rows), rows)],
            dq_in.at[h, z], dq_send.at[h], dq_recv.at[h])

        for kb in range(nk // TILE):
            at = kb * TILE
            both = nn_dot(wd16[2 * at:2 * (at + TILE), :], qx[...])
            for part in range(TILE // rows):
                here = slice(at + part * rows, at + (part + 1) * rows)
                grad_v = both[2 * part * rows:(2 * part + 1) * rows, :LANES]
                grad_k = both[(2 * part + 1) * rows:(2 * part + 2) * rows]
                dkv_out[h, here, :] = jnp.where(low_lane, grad_k[:, :LANES], grad_v).astype(BF16)
                col_emb[here, :] += gain * grad_k[:, LANES:]
            if final:
                here = slice(at, at + TILE)
                col_t = jnp.transpose(col_emb[here, :])
                emb_out[1, :, here] = (-2.0 * (
                    col_t[ONE_LANE:ONE_LANE + 1, :] * ket[64:128, here].astype(F32) - col_t[:64, :]
                )).astype(BF16)
                for part in range(TILE // rows):
                    other = kb * (TILE // rows) + part
                    here = pl.ds(at + part * rows, rows)
                    send_a(other, emb_out.at[1, :, here], emb_in.at[1, a],
                           em_send.at[1], em_recv.at[1])
                    send_a(other, dkv_out.at[h, here, :], dkv_in.at[h, a],
                           dkv_send.at[h], dkv_recv.at[h])
        if not final:
            for step in range(1, na):
                other = (a + step) % na
                pltpu.make_async_remote_copy(
                    src_ref=dkv_out.at[h, pl.ds(pl.multiple_of(other * rows, rows), rows), :],
                    dst_ref=dkv_in.at[h, a], send_sem=dkv_send.at[h], recv_sem=dkv_recv.at[h],
                    device_id=a_device(other), device_id_type=MESH).start()
        dq_in[h, z] = dq_out[h, :, pl.ds(own_q, rows)]
        dkv_in[h, a] = dkv_out[h, pl.ds(own_k, rows), :]

    def step(t, _):
        @pl.when(t < heads)
        def _():
            first_pass(t)

        @pl.when(t > 1)
        def _():
            second_pass(t - 2, False)
        return 0

    lax.fori_loop(0, heads + 1, step, 0)
    second_pass(last, True)
    emb_in[0, z] = emb_out[0, :, pl.ds(own_q, rows)]
    emb_in[1, a] = emb_out[1, :, pl.ds(own_k, rows)]

    def results_of(pair):
        cols = pl.ds(pair * LANES, LANES)
        return [
            pltpu.make_async_copy(source.at[:, cols], dest.at[:, cols], out_sem.at[pair, i])
            for i, (source, dest) in enumerate(((q_in, dq_ref), (k_in, dk_ref), (v_in, dv_ref)))
        ]

    def reduce_pair(pair):
        halves = []
        for h in (2 * pair, 2 * pair + 1):
            bytes_of(dq_in.at[h, pl.ds(0, nz - 1)], dq_recv.at[h])
            bytes_of(dkv_in.at[h, pl.ds(0, na - 1)], dkv_recv.at[h])
            halves.append((
                jnp.sum(dq_in[h].astype(F32), axis=0), jnp.sum(dkv_in[h].astype(F32), axis=0)))
        cols = slice(pair * LANES, (pair + 1) * LANES)
        (q0, kv0), (q1, kv1) = halves
        q_in[:, cols] = jnp.transpose(jnp.concatenate([q0, q1], axis=0)).astype(BF16)
        k_in[:, cols] = jnp.concatenate([kv0[:, :64], kv1[:, :64]], axis=1).astype(BF16)
        v_in[:, cols] = jnp.concatenate([kv0[:, 64:], kv1[:, 64:]], axis=1).astype(BF16)
        for copy in results_of(pair):
            copy.start()

    def gather_sent(msg):
        first, size = (64 + msg * rows, rows) if msg else (0, 64 + rows)
        bytes_of(qbuf.at[pl.ds(0, nz - 1), pl.ds(first, size), :], gz_send.at[msg])
        bytes_of(kbuf.at[pl.ds(0, na - 1), pl.ds(first, size), :], ga_send.at[msg])

    for pair in range(heads // 2 - 1):
        reduce_pair(pair)
    for h in range(heads):
        gather_sent(h)
        bytes_of(stats.at[h, pl.ds(0, nz - 1)], st_send.at[h])
    bytes_of(emb_in.at[1, pl.ds(0, na - 1)], em_recv.at[1])
    bytes_of(emb_in.at[0, pl.ds(0, nz - 1)], em_recv.at[0])
    mine = jnp.sum(emb_in[0].astype(F32), axis=0) + jnp.sum(emb_in[1].astype(F32), axis=0)
    mine = mine.astype(BF16)
    head_out[...] = mine
    for step in range(1, nh):
        pltpu.make_async_remote_copy(
            src_ref=head_out, dst_ref=head_in.at[head], send_sem=hd_send, recv_sem=hd_recv,
            device_id=(seq, (head + step) % nh), device_id_type=MESH).start()
    head_in[head] = mine
    reduce_pair(heads // 2 - 1)
    bytes_of(head_in.at[pl.ds(0, nh - 1)], hd_recv)
    total_emb[...] = jnp.sum(head_in[...].astype(F32), axis=0)
    leaving = pltpu.make_async_copy(total_emb, de_ref, in_sem.at[0])
    leaving.start()
    for h in range(heads):
        bytes_of(dq_in.at[h, pl.ds(0, nz - 1)], dq_send.at[h])
        bytes_of(dkv_in.at[h, pl.ds(0, na - 1)], dkv_send.at[h])
    bytes_of(emb_in.at[0, pl.ds(0, nz - 1)], em_send.at[0])
    bytes_of(emb_in.at[1, pl.ds(0, na - 1)], em_send.at[1])
    bytes_of(head_in.at[pl.ds(0, nh - 1)], hd_send)
    for pair in range(heads // 2):
        for copy in results_of(pair):
            copy.wait()
    leaving.wait()


def hand_over(*refs):
    for source, dest in zip(refs[:4], refs[4:]):
        dest[...] = source[...]


def on_device(na, nz, nh, query_in, key_in, value_in, grad_out, embedding, bias_gain):
    rows, width = query_in.shape
    heads = width // 64
    nq, nk = nz * rows, na * rows
    vmem = pl.BlockSpec(memory_space=pltpu.VMEM)
    dma = pltpu.SemaphoreType.DMA
    grad_q, grad_k, grad_v, grad_e = pl.pallas_call(
        functools.partial(kernel, na, nz, nh),
        out_shape=(
            jax.ShapeDtypeStruct((rows, width), BF16),
            jax.ShapeDtypeStruct((rows, width), BF16),
            jax.ShapeDtypeStruct((rows, width), BF16),
            jax.ShapeDtypeStruct((64, rows), F32),
        ),
        in_specs=[pl.BlockSpec(memory_space=pltpu.SMEM)] + [pl.BlockSpec(memory_space=pl.ANY)] * 5,
        out_specs=(pl.BlockSpec(memory_space=pl.ANY),) * 4,
        scratch_shapes=[
            pltpu.VMEM((rows, width), BF16),
            pltpu.VMEM((rows, width), BF16),
            pltpu.VMEM((rows, width), BF16),
            pltpu.VMEM((rows, width), BF16),
            pltpu.VMEM((64, rows), BF16),
            dma((5,)),
            pltpu.VMEM((64, rows), F32),
            dma((width // LANES, 3)),
            pltpu.VMEM((nz, 64 + heads * rows, LANES), BF16),
            pltpu.VMEM((na, 64 + heads * rows, LANES), BF16),
            pltpu.VMEM((nk, 2 * LANES), BF16),
            pltpu.VMEM((nq, 2 * LANES), BF16),
            pltpu.VMEM((nq, LANES), BF16),
            pltpu.VMEM((nq, 2 * LANES), BF16),
            pltpu.VMEM((64 + EMB_ROWS, nk), BF16),
            pltpu.VMEM((LANES, nq), F32),
            pltpu.VMEM((nq, LANES), F32),
            pltpu.VMEM((nq, LANES), BF16),
            pltpu.VMEM((nk, LANES), BF16),
            pltpu.VMEM((SLOTS, nk, nq), F32),
            pltpu.VMEM((SLOTS, nk, nq), F32),
            pltpu.VMEM((2 * nk, nq), BF16),
            pltpu.VMEM((SLOTS, na, nq), F32),
            pltpu.VMEM((na, 8, nq), F32),
            pltpu.VMEM((na, 8, nq), F32),
            pltpu.VMEM((na, nq), F32),
            pltpu.VMEM((heads, nz, 16, LANES), F32),
            pltpu.VMEM((16, LANES), F32),
            pltpu.VMEM((EMB_ROWS, nq), F32),
            pltpu.VMEM((nk, LANES), F32),
            pltpu.VMEM((heads, 64, nq), BF16),
            pltpu.VMEM((heads, nk, LANES), BF16),
            pltpu.VMEM((heads, nz, 64, rows), BF16),
            pltpu.VMEM((heads, na, rows, LANES), BF16),
            pltpu.VMEM((2, 64, max(nq, nk)), BF16),
            pltpu.VMEM((2, max(na, nz), 64, rows), BF16),
            pltpu.VMEM((64, rows), BF16),
            pltpu.VMEM((nh, 64, rows), BF16),
            dma((heads,)), dma((heads, nz)),
            dma((heads,)), dma((heads, na)),
            dma((heads,)), dma((heads,)),
            dma((heads,)), dma((heads,)),
            dma((heads,)), dma((heads,)),
            dma((2,)), dma((2,)),
            dma, dma,
        ],
        compiler_params=pltpu.CompilerParams(
            collective_id=0, has_side_effects=True, vmem_limit_bytes=56 * 1024 * 1024
        ),
    )(bias_gain, query_in, key_in, value_in, grad_out, embedding.T)
    results = (grad_q, grad_k, grad_v, grad_e)
    grad_q, grad_k, grad_v, grad_e = pl.pallas_call(
        hand_over,
        out_shape=tuple(jax.ShapeDtypeStruct(r.shape, r.dtype) for r in results),
        in_specs=[vmem] * 4,
        out_specs=(vmem,) * 4,
    )(*results)
    return grad_q, grad_k, grad_v, grad_e.T


def solution(mesh):
    seq, nh = mesh.shape["seq"], mesh.shape["head"]
    nz = 1
    while nz * nz < seq:
        nz *= 2
    na = seq // nz
    placed = (
        P("seq", "head"),
        P("seq", "head"),
        P("seq", "head"),
        P("seq", "head"),
        P("seq", None),
        P("head"),
    )
    return jax.shard_map(
        functools.partial(on_device, na, nz, nh),
        mesh=mesh,
        in_specs=placed,
        out_specs=(P("seq", "head"), P("seq", "head"), P("seq", "head"), P("seq", None)),
        check_vma=False,
    )
```

```python
import functools

import jax
import jax.numpy as jnp
from jax import lax
from jax.experimental import pallas as pl
from jax.experimental.pallas import tpu as pltpu
from jax.sharding import PartitionSpec as P

MESH = pl.DeviceIdType.MESH
F32 = jnp.float32
BF16 = jnp.bfloat16
LANES = 128
TILE = 256
ONE_LANE = 76
SLOTS = 3
EMB_ROWS = 80


def nt_dot(left, right):
    return lax.dot_general(left, right, (((1,), (1,)), ((), ())), preferred_element_type=F32)


def nn_dot(left, right):
    return jnp.dot(left, right, preferred_element_type=F32)


def rounded(x):
    return x.astype(BF16).astype(F32)


def three_parts(x):
    first = rounded(x)
    second = rounded(x - first)
    return first, second, rounded(x - first - second)


def gain_pattern(base, gain):
    lane = lax.broadcasted_iota(jnp.int32, (1, LANES), 1) - base
    one, two, three = three_parts(jnp.full((1, LANES), gain, F32))
    out = jnp.where((lane == 0) | (lane == 3) | (lane == 5), -one, 0.0)
    out = jnp.where((lane == 1) | (lane == 4), -two, out)
    return jnp.where(lane == 2, -three, out)


Z_FIRST = ((0, 2, 2, 0), (0, -2, 6, 0), (0, 1, 1, 0), (0, -1, 7, 0))
Z_AHEAD = ((-2, 2, 4, 1), (-2, 1, 3, 0))
Z_BACK = ((2, -2, 0, 2), (2, -1, 5, 0))
FAR_FIRST = (4, 3, 5, 2, 6, 1, 7)


def kernel(
    na, nz, nh,
    gain_ref, q_ref, k_ref, v_ref, g_ref, emb_ref,
    dq_ref, dk_ref, dv_ref, de_ref,
    q_in, k_in, v_in, g_in, emb_in_place, in_sem, total_emb, out_sem,
    qbuf, kbuf, ka, qa, gq, qx, ket, eqt, twice_q, tail_q, tail_k,
    scores, probs, wd16, block_max, totals, moments, shares, stats, combined,
    row_emb, col_emb, dq_out, dkv_out, dq_in, dkv_in,
    emb_out, emb_in, head_out, head_in,
    gz_send, gz_recv, ga_send, ga_recv, st_send, st_recv,
    dq_send, dq_recv, dkv_send, dkv_recv, em_send, em_recv, hd_send, hd_recv,
):
    rows = q_ref.shape[0]
    heads = q_ref.shape[1] // 64
    nq, nk = nz * rows, na * rows
    nx = na // 2
    last = heads - 1
    seq, head = lax.axis_index("seq"), lax.axis_index("head")
    a, z = seq // nz, seq % nz
    y, x = a // nx, a % nx
    own_q = pl.multiple_of(z * rows, rows)
    own_k = pl.multiple_of(a * rows, rows)

    def z_at(step):
        return (z + step + nz) % nz

    def z_device(place):
        return (a * nz + place, head)

    def a_device(place):
        return (place * nz + z, head)

    loads = [
        pltpu.make_async_copy(source, dest, in_sem.at[i])
        for i, (source, dest) in enumerate((
            (emb_ref, emb_in_place), (q_ref, q_in), (g_ref, g_in), (k_ref, k_in), (v_ref, v_in)))
    ]
    for load in loads:
        load.start()

    barrier = pltpu.get_barrier_semaphore()

    def greet(target):
        pl.semaphore_signal(barrier, inc=1, device_id=target, device_id_type=MESH)

    for step in range(1, nz):
        greet(z_device(z_at(step)))
    for step in range(1, na):
        greet(a_device((a + step) % na))
    for step in range(1, nh):
        greet((seq, (head + step) % nh))

    def head_rows(h):
        return pl.ds(pl.multiple_of(64 + h * rows, 64), rows)

    def packed(left, right, h, scale):
        cols = slice(h * 64, (h + 1) * 64)
        return jnp.concatenate(
            [left[:, cols].astype(F32) * scale, right[:, cols].astype(F32)], axis=1).astype(BF16)

    def pack_head(h):
        qbuf[z, head_rows(h), :] = packed(q_in, g_in, h, 0.125)
        kbuf[a, head_rows(h), :] = packed(k_in, v_in, h, 1.0)

    for load in loads:
        load.wait()
    qbuf[z, 0:64, :] = emb_in_place[...]
    kbuf[a, 0:64, :] = emb_in_place[...]
    pack_head(0)

    pl.semaphore_wait(barrier, (nz - 1) + (na - 1) + (nh - 1))

    def piece(msg, buffer, place, part):
        if isinstance(msg, int) and msg == 0:
            first, size = 0, 64 + rows
        else:
            first, size = pl.multiple_of(64 + msg * rows, 64), rows
        if part:
            size = size // 2
            first = first + (size if part == 2 else 0)
        return buffer.at[place, pl.ds(first, size), :]

    def z_send(msg, plan):
        for held, to, slot, part in plan:
            block = piece(msg, qbuf, z_at(held), part)
            pltpu.make_async_remote_copy(
                src_ref=block, dst_ref=block,
                send_sem=gz_send.at[msg], recv_sem=gz_recv.at[msg, slot],
                device_id=z_device(z_at(to)), device_id_type=MESH).start()

    def z_wait(msg, slot):
        block = piece(msg, qbuf, z_at(-4 if slot == 0 else -slot), {0: 2, 4: 1}.get(slot, 0))
        pltpu.make_async_copy(block, block, gz_recv.at[msg, slot]).wait()

    def a_send(msg, partner):
        held = ((y + partner) % 2) * nx + x
        block = piece(msg, kbuf, held, 0)
        targets = [] if partner else [(4, ((y + 1) % 2) * nx + x)]
        targets += [(4 * partner + step, y * nx + (x + step) % nx) for step in (2, 1, 3)]
        for slot, place in targets:
            pltpu.make_async_remote_copy(
                src_ref=block, dst_ref=block,
                send_sem=ga_send.at[msg], recv_sem=ga_recv.at[msg, slot],
                device_id=a_device(place), device_id_type=MESH).start()

    def a_wait(msg, slot):
        held = ((y + slot // 4) % 2) * nx + (x - slot % 4 + nx) % nx
        block = piece(msg, kbuf, held, 0)
        pltpu.make_async_copy(block, block, ga_recv.at[msg, slot]).wait()

    def gather_start(msg):
        z_send(msg, Z_FIRST[:2])
        a_send(msg, 0)
        z_send(msg, Z_FIRST[2:])

    def gather_forward(msg):
        a_wait(msg, 4)
        a_send(msg, 1)
        z_wait(msg, 2)
        z_send(msg, Z_AHEAD)
        z_wait(msg, 6)
        z_send(msg, Z_BACK)

    def gather_end(msg):
        for slot in (1, 7, 3, 5, 4, 0):
            z_wait(msg, slot)
        for slot in (1, 3, 2, 5, 7, 6):
            a_wait(msg, slot)

    def spread_z(source, dest, send_sem, recv_sem):
        for step in FAR_FIRST:
            other = z_at(step)
            pltpu.make_async_remote_copy(
                src_ref=source(other), dst_ref=dest, send_sem=send_sem, recv_sem=recv_sem,
                device_id=z_device(other), device_id_type=MESH).start()

    def send_a(other, source, dest, send_sem, recv_sem):
        @pl.when(other != a)
        def _():
            pltpu.make_async_remote_copy(
                src_ref=source, dst_ref=dest, send_sem=send_sem, recv_sem=recv_sem,
                device_id=a_device(other), device_id_type=MESH).start()

    def bytes_of(block, sem):
        pltpu.make_async_copy(block, block, sem).wait()

    gather_start(0)
    pack_head(1)
    gather_start(1)
    for h in range(2, heads):
        pack_head(h)
    row_emb[...] = jnp.zeros_like(row_emb)
    col_emb[...] = jnp.zeros_like(col_emb)
    gather_forward(0)
    gather_start(2)
    gather_forward(1)
    gather_start(3)
    gather_end(0)

    def of_queries(h):
        return qbuf[:, head_rows(h), :].reshape(nq, LANES)

    def of_keys(h):
        return kbuf[:, head_rows(h), :].reshape(nk, LANES)

    def widened(emb_t, base):
        e = emb_t.astype(F32)
        one, two, three = three_parts(jnp.sum(e * e, axis=0, keepdims=True))
        row = lax.broadcasted_iota(jnp.int32, (16, e.shape[1]), 0) + (64 - base)
        extra = jnp.where((row >= 0) & (row < 3), one, 0.0)
        extra = jnp.where((row >= 3) & (row < 5), two, extra)
        extra = jnp.where(row == 5, three, extra)
        extra = jnp.where(row == ONE_LANE - base, 1.0, extra)
        return jnp.concatenate([e, extra, jnp.zeros((48, e.shape[1]), F32)], axis=0)

    low_lane = lax.broadcasted_iota(jnp.int32, (1, LANES), 1) < 64
    low_f32 = jnp.where(low_lane, 1.0, 0.0)
    high_f32 = 1.0 - low_f32
    low_16, high_16 = low_f32.astype(BF16), high_f32.astype(BF16)
    one_lane = jnp.where(lax.broadcasted_iota(jnp.int32, (1, LANES), 1) == ONE_LANE, 1.0, 0.0)

    eqt[...] = widened(jnp.concatenate([qbuf[i, 0:64, :] for i in range(nz)], axis=1), 64)
    wide_k = widened(jnp.concatenate([kbuf[i, 0:64, :] for i in range(na)], axis=1), 70)
    ket[64:, :] = wide_k[:EMB_ROWS].astype(BF16)
    wide_q = jnp.transpose(eqt[...])
    wide_k = jnp.transpose(wide_k)
    qx[:, LANES:] = wide_q.astype(BF16)
    tail_q[...] = (wide_q * high_f32).astype(BF16)
    tail_k[...] = ((wide_k - one_lane) * high_f32).astype(BF16)
    wide_q, wide_k = wide_q * low_f32, wide_k * low_f32
    twice_q[...] = wide_q + pltpu.roll(wide_q, 64, 1)
    ka[:, LANES:] = (wide_k + pltpu.roll(wide_k, 64, 1)).astype(BF16)

    def first_pass(h):
        slot = h % SLOTS
        @pl.when(h > 0)
        def _():
            gather_end(h)

        gain = gain_ref[h]
        ka[:, :LANES] = of_keys(h) * low_16 + (tail_k[...] + gain_pattern(64, gain).astype(BF16))
        qa[:, :LANES] = of_queries(h) * low_16 + (tail_q[...] + gain_pattern(70, gain).astype(BF16))
        scaled = twice_q[...] * (2.0 * gain)
        first = rounded(scaled)
        qa[:, LANES:] = jnp.where(low_lane, first, scaled - first).astype(BF16)
        gq[...] = of_queries(h) * high_16

        def block(qb):
            at = slice(qb * TILE, (qb + 1) * TILE)
            q_tile, g_tile = qa[at, :], gq[at, :]
            for kb in range(na):
                keys = slice(kb * rows, (kb + 1) * rows)
                s = nt_dot(ka[keys, :], q_tile)
                p = nt_dot(kbuf[kb, head_rows(h), :], g_tile)
                top = jnp.max(jnp.max(s.reshape(rows // 8, 8, TILE), axis=0), axis=0, keepdims=True)
                e = jnp.exp(s - top)
                scores[slot, keys, at] = e
                probs[slot, keys, at] = p
                block_max[slot, kb:kb + 1, at] = top
                totals[kb, :, at] = jnp.sum(e.reshape(rows // 8, 8, TILE), axis=0)
                moments[kb, :, at] = jnp.sum((e * p).reshape(rows // 8, 8, TILE), axis=0)

        for qb in range(nq // TILE):
            block(qb)
            if qb == 1:
                @pl.when(h < last - 1)
                def _():
                    gather_forward(h + 2)

        top = jnp.max(block_max[slot], axis=0, keepdims=True)
        share = jnp.exp(block_max[slot] - top)
        total = sum(totals[kb] * share[kb:kb + 1] for kb in range(na))
        moment = sum(moments[kb] * share[kb:kb + 1] for kb in range(na))
        total = jnp.sum(total, axis=0, keepdims=True)
        moment = jnp.sum(moment, axis=0, keepdims=True) / total
        log_sum = top + jnp.log(total)
        for row in range(nz):
            cols = slice(row * rows, (row + 1) * rows)
            stats[h, z, row:row + 1, :] = log_sum[:, cols]
            stats[h, z, row + 8:row + 9, :] = moment[:, cols]
        own = stats.at[h, z]
        spread_z(lambda other: own, own, st_send.at[h], st_recv.at[h])

    def second_pass(h, final):
        slot = h % SLOTS
        gain = gain_ref[h]
        qx[:, :LANES] = of_queries(h)
        ket[:64, :] = jnp.transpose(of_keys(h).astype(F32))[:64].astype(BF16)
        bytes_of(stats.at[h, pl.ds(0, nz - 1)], st_recv.at[h])
        top = stats[h, 0, 0:8, :]
        for other in range(1, nz):
            top = jnp.maximum(top, stats[h, other, 0:8, :])
        total = jnp.zeros((8, LANES), F32)
        moment = jnp.zeros((8, LANES), F32)
        for other in range(nz):
            share = jnp.exp(stats[h, other, 0:8, :] - top)
            total = total + share
            moment = moment + stats[h, other, 8:16, :] * share
        combined[0:8, :] = top + jnp.log(total)
        combined[8:16, :] = moment / total

        log_total = jnp.concatenate([combined[row:row + 1, :] for row in range(nz)], axis=1)
        delta_row = jnp.concatenate([combined[8 + row:9 + row, :] for row in range(nz)], axis=1)
        shares[...] = jnp.exp(block_max[slot] - log_total)

        def query_block(qb):
            at = slice(qb * TILE, (qb + 1) * TILE)
            delta = delta_row[:, at]
            for kb in range(na):
                keys = slice(kb * rows, (kb + 1) * rows)
                w = scores[slot, keys, at] * shares[kb:kb + 1, at]
                d = w * (probs[slot, keys, at] - delta)
                wd16[2 * kb * rows:(2 * kb + 1) * rows, at] = w.astype(BF16)
                wd16[(2 * kb + 1) * rows:(2 * kb + 2) * rows, at] = d.astype(BF16)
            dqt = jnp.zeros((64 + EMB_ROWS, TILE), F32)
            for kb in range(nk // TILE):
                d_tile = jnp.concatenate([
                    wd16[(2 * b + 1) * rows:(2 * b + 2) * rows, at]
                    for b in range(kb * TILE // rows, (kb + 1) * TILE // rows)], axis=0)
                dqt = dqt + nn_dot(ket[:, kb * TILE:(kb + 1) * TILE], d_tile)
            row_emb[:, at] += gain * dqt[64:, :]
            dq_out[h, :, at] = (dqt[:64, :] * 0.125).astype(BF16)

        for qb in range(nq // TILE):
            query_block(qb)
        if final:
            emb_out[0] = (-2.0 * (
                row_emb[ONE_LANE:ONE_LANE + 1, :] * eqt[:64, :] - row_emb[:64, :]
            )).astype(BF16)
            spread_z(
                lambda other: emb_out.at[0, :, pl.ds(pl.multiple_of(other * rows, rows), rows)],
                emb_in.at[0, z], em_send.at[0], em_recv.at[0])
        spread_z(
            lambda other: dq_out.at[h, :, pl.ds(pl.multiple_of(other * rows, rows), rows)],
            dq_in.at[h, z], dq_send.at[h], dq_recv.at[h])

        for kb in range(nk // TILE):
            at = kb * TILE
            both = nn_dot(wd16[2 * at:2 * (at + TILE), :], qx[...])
            for part in range(TILE // rows):
                here = slice(at + part * rows, at + (part + 1) * rows)
                grad_v = both[2 * part * rows:(2 * part + 1) * rows, :LANES]
                grad_k = both[(2 * part + 1) * rows:(2 * part + 2) * rows]
                dkv_out[h, here, :] = jnp.where(low_lane, grad_k[:, :LANES], grad_v).astype(BF16)
                col_emb[here, :] += gain * grad_k[:, LANES:]
            if final:
                here = slice(at, at + TILE)
                col_t = jnp.transpose(col_emb[here, :])
                emb_out[1, :, here] = (-2.0 * (
                    col_t[ONE_LANE:ONE_LANE + 1, :] * ket[64:128, here].astype(F32) - col_t[:64, :]
                )).astype(BF16)
                for part in range(TILE // rows):
                    other = kb * (TILE // rows) + part
                    here = pl.ds(at + part * rows, rows)
                    send_a(other, emb_out.at[1, :, here], emb_in.at[1, a],
                           em_send.at[1], em_recv.at[1])
                    send_a(other, dkv_out.at[h, here, :], dkv_in.at[h, a],
                           dkv_send.at[h], dkv_recv.at[h])
        if not final:
            for step in range(1, na):
                other = (a + step) % na
                pltpu.make_async_remote_copy(
                    src_ref=dkv_out.at[h, pl.ds(pl.multiple_of(other * rows, rows), rows), :],
                    dst_ref=dkv_in.at[h, a], send_sem=dkv_send.at[h], recv_sem=dkv_recv.at[h],
                    device_id=a_device(other), device_id_type=MESH).start()
        dq_in[h, z] = dq_out[h, :, pl.ds(own_q, rows)]
        dkv_in[h, a] = dkv_out[h, pl.ds(own_k, rows), :]

    def step(t, _):
        @pl.when(t < heads)
        def _():
            first_pass(t)

        @pl.when(t > 1)
        def _():
            second_pass(t - 2, False)
        return 0

    lax.fori_loop(0, heads + 1, step, 0)
    second_pass(last, True)
    emb_in[0, z] = emb_out[0, :, pl.ds(own_q, rows)]
    emb_in[1, a] = emb_out[1, :, pl.ds(own_k, rows)]

    def results_of(pair):
        cols = pl.ds(pair * LANES, LANES)
        return [
            pltpu.make_async_copy(source.at[:, cols], dest.at[:, cols], out_sem.at[pair, i])
            for i, (source, dest) in enumerate(((q_in, dq_ref), (k_in, dk_ref), (v_in, dv_ref)))
        ]

    def reduce_pair(pair):
        halves = []
        for h in (2 * pair, 2 * pair + 1):
            bytes_of(dq_in.at[h, pl.ds(0, nz - 1)], dq_recv.at[h])
            bytes_of(dkv_in.at[h, pl.ds(0, na - 1)], dkv_recv.at[h])
            halves.append((
                jnp.sum(dq_in[h].astype(F32), axis=0), jnp.sum(dkv_in[h].astype(F32), axis=0)))
        cols = slice(pair * LANES, (pair + 1) * LANES)
        (q0, kv0), (q1, kv1) = halves
        q_in[:, cols] = jnp.transpose(jnp.concatenate([q0, q1], axis=0)).astype(BF16)
        k_in[:, cols] = jnp.concatenate([kv0[:, :64], kv1[:, :64]], axis=1).astype(BF16)
        v_in[:, cols] = jnp.concatenate([kv0[:, 64:], kv1[:, 64:]], axis=1).astype(BF16)
        for copy in results_of(pair):
            copy.start()

    def gather_sent(msg):
        first, size = (64 + msg * rows, rows) if msg else (0, 64 + rows)
        bytes_of(qbuf.at[pl.ds(0, nz - 1), pl.ds(first, size), :], gz_send.at[msg])
        bytes_of(kbuf.at[pl.ds(0, na - 1), pl.ds(first, size), :], ga_send.at[msg])

    for pair in range(heads // 2 - 1):
        reduce_pair(pair)
    for h in range(heads):
        gather_sent(h)
        bytes_of(stats.at[h, pl.ds(0, nz - 1)], st_send.at[h])
    bytes_of(emb_in.at[1, pl.ds(0, na - 1)], em_recv.at[1])
    bytes_of(emb_in.at[0, pl.ds(0, nz - 1)], em_recv.at[0])
    mine = jnp.sum(emb_in[0].astype(F32), axis=0) + jnp.sum(emb_in[1].astype(F32), axis=0)
    mine = mine.astype(BF16)
    head_out[...] = mine
    for step in range(1, nh):
        pltpu.make_async_remote_copy(
            src_ref=head_out, dst_ref=head_in.at[head], send_sem=hd_send, recv_sem=hd_recv,
            device_id=(seq, (head + step) % nh), device_id_type=MESH).start()
    head_in[head] = mine
    reduce_pair(heads // 2 - 1)
    bytes_of(head_in.at[pl.ds(0, nh - 1)], hd_recv)
    total_emb[...] = jnp.sum(head_in[...].astype(F32), axis=0)
    leaving = pltpu.make_async_copy(total_emb, de_ref, in_sem.at[0])
    leaving.start()
    for h in range(heads):
        bytes_of(dq_in.at[h, pl.ds(0, nz - 1)], dq_send.at[h])
        bytes_of(dkv_in.at[h, pl.ds(0, na - 1)], dkv_send.at[h])
    bytes_of(emb_in.at[0, pl.ds(0, nz - 1)], em_send.at[0])
    bytes_of(emb_in.at[1, pl.ds(0, na - 1)], em_send.at[1])
    bytes_of(head_in.at[pl.ds(0, nh - 1)], hd_send)
    for pair in range(heads // 2):
        for copy in results_of(pair):
            copy.wait()
    leaving.wait()


def hand_over(*refs):
    for source, dest in zip(refs[:4], refs[4:]):
        dest[...] = source[...]


def on_device(na, nz, nh, query_in, key_in, value_in, grad_out, embedding, bias_gain):
    rows, width = query_in.shape
    heads = width // 64
    nq, nk = nz * rows, na * rows
    vmem = pl.BlockSpec(memory_space=pltpu.VMEM)
    dma = pltpu.SemaphoreType.DMA
    grad_q, grad_k, grad_v, grad_e = pl.pallas_call(
        functools.partial(kernel, na, nz, nh),
        out_shape=(
            jax.ShapeDtypeStruct((rows, width), BF16),
            jax.ShapeDtypeStruct((rows, width), BF16),
            jax.ShapeDtypeStruct((rows, width), BF16),
            jax.ShapeDtypeStruct((64, rows), F32),
        ),
        in_specs=[pl.BlockSpec(memory_space=pltpu.SMEM)] + [pl.BlockSpec(memory_space=pl.ANY)] * 5,
        out_specs=(pl.BlockSpec(memory_space=pl.ANY),) * 4,
        scratch_shapes=[
            pltpu.VMEM((rows, width), BF16),
            pltpu.VMEM((rows, width), BF16),
            pltpu.VMEM((rows, width), BF16),
            pltpu.VMEM((rows, width), BF16),
            pltpu.VMEM((64, rows), BF16),
            dma((5,)),
            pltpu.VMEM((64, rows), F32),
            dma((width // LANES, 3)),
            pltpu.VMEM((nz, 64 + heads * rows, LANES), BF16),
            pltpu.VMEM((na, 64 + heads * rows, LANES), BF16),
            pltpu.VMEM((nk, 2 * LANES), BF16),
            pltpu.VMEM((nq, 2 * LANES), BF16),
            pltpu.VMEM((nq, LANES), BF16),
            pltpu.VMEM((nq, 2 * LANES), BF16),
            pltpu.VMEM((64 + EMB_ROWS, nk), BF16),
            pltpu.VMEM((LANES, nq), F32),
            pltpu.VMEM((nq, LANES), F32),
            pltpu.VMEM((nq, LANES), BF16),
            pltpu.VMEM((nk, LANES), BF16),
            pltpu.VMEM((SLOTS, nk, nq), F32),
            pltpu.VMEM((SLOTS, nk, nq), F32),
            pltpu.VMEM((2 * nk, nq), BF16),
            pltpu.VMEM((SLOTS, na, nq), F32),
            pltpu.VMEM((na, 8, nq), F32),
            pltpu.VMEM((na, 8, nq), F32),
            pltpu.VMEM((na, nq), F32),
            pltpu.VMEM((heads, nz, 16, LANES), F32),
            pltpu.VMEM((16, LANES), F32),
            pltpu.VMEM((EMB_ROWS, nq), F32),
            pltpu.VMEM((nk, LANES), F32),
            pltpu.VMEM((heads, 64, nq), BF16),
            pltpu.VMEM((heads, nk, LANES), BF16),
            pltpu.VMEM((heads, nz, 64, rows), BF16),
            pltpu.VMEM((heads, na, rows, LANES), BF16),
            pltpu.VMEM((2, 64, max(nq, nk)), BF16),
            pltpu.VMEM((2, max(na, nz), 64, rows), BF16),
            pltpu.VMEM((64, rows), BF16),
            pltpu.VMEM((nh, 64, rows), BF16),
            dma((heads,)), dma((heads, nz)),
            dma((heads,)), dma((heads, na)),
            dma((heads,)), dma((heads,)),
            dma((heads,)), dma((heads,)),
            dma((heads,)), dma((heads,)),
            dma((2,)), dma((2,)),
            dma, dma,
        ],
        compiler_params=pltpu.CompilerParams(
            collective_id=0, has_side_effects=True, vmem_limit_bytes=56 * 1024 * 1024
        ),
    )(bias_gain, query_in, key_in, value_in, grad_out, embedding.T)
    results = (grad_q, grad_k, grad_v, grad_e)
    grad_q, grad_k, grad_v, grad_e = pl.pallas_call(
        hand_over,
        out_shape=tuple(jax.ShapeDtypeStruct(r.shape, r.dtype) for r in results),
        in_specs=[vmem] * 4,
        out_specs=(vmem,) * 4,
    )(*results)
    return grad_q, grad_k, grad_v, grad_e.T


def solution(mesh):
    seq, nh = mesh.shape["seq"], mesh.shape["head"]
    nz = 1
    while nz * nz < seq:
        nz *= 2
    na = seq // nz
    placed = (
        P("seq", "head"),
        P("seq", "head"),
        P("seq", "head"),
        P("seq", "head"),
        P("seq", None),
        P("head"),
    )
    return jax.shard_map(
        functools.partial(on_device, na, nz, nh),
        mesh=mesh,
        in_specs=placed,
        out_specs=(P("seq", "head"), P("seq", "head"), P("seq", "head"), P("seq", None)),
        check_vma=False,
    )
```
